32 devices in a mesh: vel: 4 (over x, core), sx: 2 (over y), sy: 4 (over z).
Axes of the slice: x: 2, y: 2, z: 4, core: 2. Of those that a mesh axis runs over, the one named last changes fastest.
Arguments:
- distribution: bfloat16 [6, 128, 32768], P('sx', 'sy', 'vel'), may hold values from 0.05 to 5, as said below
- plane_weights: bfloat16 [1024, 1024], P(('sx', 'sy')), may hold values from -0.1875 to 0.1875
- depth_weights: bfloat16 [32, 32], replicated, may hold values from -1 to 1
Outputs:
- advanced: bfloat16 [6, 128, 32768], P('sx', 'sy', 'vel')
The draws below stay inside these ranges and needn't reach their ends.
Inputs may be any that keep to these rules, and one draw needn't show every extreme that they name: `distribution`: every entry is positive.
All inputs are finite; a program needn't handle non-finite values.
Results may differ from the reference program's by a relative error of at most 0.0028.
Values may be sent and summed in bfloat16 or wider, within the bound.
A program may use at most 64 MiB of HBM per device.

```python
import math
import jax
import jax.numpy as jnp
from jax import lax

NVZ = 32
NVX = 32
NVY = 32
NXY = 1024
NVEL = 32768
NROWS = 6
NCOLS = 128


def draw_distribution(key, part):
    full_shape = (NROWS, NCOLS, NVEL)
    depth_share = (jnp.arange(NVEL, dtype=jnp.int32) // (NVX * NVY)).astype(jnp.float32) / (NVZ - 1)
    roughness = jax.random.uniform(key, full_shape, jnp.float32, 0.5, 1.5)
    growth = jnp.exp(math.log(3.0) * depth_share)
    return (roughness * growth).astype(jnp.bfloat16)


def levels(key, dims, shards, low, top_value):
    level, own = 1.0, jax.random.fold_in(key, 6)
    for dim, blocks in shards:
        steps = jnp.exp(jax.random.uniform(jax.random.fold_in(own, dim), (blocks,), jnp.float32, low / len(shards), top_value / len(shards)))
        level = level * jnp.repeat(steps, dims[dim] // blocks).reshape([-1 if axis == dim else 1 for axis in range(len(dims))])
    return level


def normal_values(own_key, extent, scale, limit, cuts=(), kind=jnp.bfloat16):
    drawn = scale * jax.random.normal(own_key, extent, jnp.float32)
    if cuts:
        drawn = drawn * levels(own_key, extent, cuts, -0.22, 0.18)
    return jnp.clip(drawn, -limit, limit).astype(kind)


def setup_inputs(seed: int = 0) -> dict:
    seeds = jax.random.split(jax.random.key(seed), 4)
    distribution = draw_distribution(jax.random.fold_in(seeds[3], 71), 0)
    plane_weights = normal_values(seeds[1], (NXY, NXY), NXY ** -0.5, 0.1875, ((0, 8),))
    depth_weights = normal_values(seeds[2], (NVZ, NVZ), NVZ ** -0.5, 1.0)
    return {"distribution": distribution, "plane_weights": plane_weights, "depth_weights": depth_weights}


COURANT = 0.45
RELAX_RATE = 0.3


def plane_speeds():
    lane_ids = jnp.arange(NVX * NVY, dtype=jnp.int32)
    speed_across = ((lane_ids // NVY).astype(jnp.float32) - (NVX - 1) / 2.0) * (8.0 / NVX)
    speed_along = ((lane_ids % NVY).astype(jnp.float32) - (NVY - 1) / 2.0) * (8.0 / NVY)
    return speed_across, speed_along


def maxwellian(particle_concentration, momentum_across, momentum_along, momentum_depth, motion_work_content, speed_across, speed_along, speed_depth):
    mean_flow_transverse = momentum_across / particle_concentration
    mean_flow_streamwise = momentum_along / particle_concentration
    mean_flow_vertical = momentum_depth / particle_concentration
    cell_heat_level = (motion_work_content / particle_concentration - (mean_flow_transverse ** 2 + mean_flow_streamwise ** 2 + mean_flow_vertical ** 2)) / 3.0
    speed_grid_cell_measure = (8.0 / NVX) * (8.0 / NVY) * (8.0 / NVZ)
    scaling_divisor = particle_concentration * speed_grid_cell_measure / (2.0 * jnp.pi * cell_heat_level) ** 1.5
    maxwellian_width = (speed_across - mean_flow_transverse[:, None, None]) ** 2
    maxwellian_width = maxwellian_width + (speed_along - mean_flow_streamwise[:, None, None]) ** 2
    maxwellian_width = maxwellian_width + (speed_depth[:, None] - mean_flow_vertical[:, None, None]) ** 2
    return scaling_divisor[:, None, None] * jnp.exp(-maxwellian_width / (2.0 * cell_heat_level[:, None, None]))


def reference(distribution, plane_weights, depth_weights):
    speed_across, speed_along = plane_speeds()
    speed_depth = (jnp.arange(NVZ, dtype=jnp.int32).astype(jnp.float32) - (NVZ - 1) / 2.0) * (8.0 / NVZ)
    lanes_total = NVX * NVY
    lattice = distribution.reshape(NROWS, NCOLS, NVZ, lanes_total)
    depth_float = depth_weights.astype(jnp.float32)
    squared = speed_across ** 2 + speed_along ** 2 + speed_depth[:, None] ** 2
    courant_across = COURANT / (4.0 - 4.0 / NVX)
    courant_along = COURANT / (4.0 - 4.0 / NVY)

    def one_row(row_index):
        current = lax.dynamic_index_in_dim(lattice, row_index, 0, keepdims=False).astype(jnp.float32)
        lower_row = lax.dynamic_index_in_dim(lattice, (row_index + NROWS - 1) % NROWS, 0, keepdims=False).astype(jnp.float32)
        upper_row = lax.dynamic_index_in_dim(lattice, (row_index + 1) % NROWS, 0, keepdims=False).astype(jnp.float32)
        particle_concentration = jnp.sum(current, axis=(1, 2))
        momentum_across = jnp.sum(current * speed_across, axis=(1, 2))
        momentum_along = jnp.sum(current * speed_along, axis=(1, 2))
        momentum_depth = jnp.sum(current * speed_depth[:, None], axis=(1, 2))
        motion_work_content = jnp.sum(current * squared, axis=(1, 2))
        equilibrium = maxwellian(particle_concentration, momentum_across, momentum_along, momentum_depth, motion_work_content, speed_across, speed_along, speed_depth)
        deviation = (equilibrium - current).astype(jnp.bfloat16)
        mixed_plane = jnp.dot(deviation.reshape(-1, lanes_total), plane_weights.T, preferred_element_type=jnp.float32)
        mixed_plane = lax.optimization_barrier(mixed_plane.astype(jnp.bfloat16)).astype(jnp.float32)
        mixed_plane = mixed_plane.reshape(NCOLS, NVZ, lanes_total)
        collision = jnp.einsum("zw,cwk->czk", depth_float, mixed_plane, precision=lax.Precision.HIGHEST)
        collision = lax.optimization_barrier(collision.astype(jnp.bfloat16)).astype(jnp.float32)
        left_column = jnp.roll(current, 1, axis=0)
        right_column = jnp.roll(current, -1, axis=0)
        across = jnp.maximum(speed_across, 0.0) * (current - lower_row) + jnp.minimum(speed_across, 0.0) * (upper_row - current)
        along = jnp.maximum(speed_along, 0.0) * (current - left_column) + jnp.minimum(speed_along, 0.0) * (right_column - current)
        advanced = current - (courant_across * across + courant_along * along) + RELAX_RATE * collision
        return advanced.astype(jnp.bfloat16)

    all_rows = lax.map(one_row, jnp.arange(NROWS, dtype=jnp.int32))
    return all_rows.reshape(NROWS, NCOLS, NVZ * lanes_total)
```

```python
import functools
import math

import jax
import jax.numpy as jnp
from jax import lax
from jax.experimental import pallas as pl
from jax.experimental.pallas import tpu as pltpu
from jax.sharding import PartitionSpec as P

NVZ = 32
NVX = 32
NVY = 32
NXY = NVX * NVY
HALF = NXY // 2
GROUP = 16
COURANT = 0.45
RELAX_RATE = 0.3
MESH = pl.DeviceIdType.MESH
F32 = jnp.float32
BF16 = jnp.bfloat16


def lane_speeds(shape, dim):
    lane = lax.broadcasted_iota(jnp.int32, shape, dim)
    across = ((lane >> 5).astype(F32) - (NVX - 1) / 2.0) * (8.0 / NVX)
    along = ((lane & 31).astype(F32) - (NVY - 1) / 2.0) * (8.0 / NVY)
    return across, along


def kernel(
    sizes, f_hbm, w_hbm, d_ref, out_hbm,
    tiles, weights, base, mixed, result, spread, probes,
    row_out, row_in, col_out, col_in, col_wide,
    loc_sem, wloc_sem, x_send, x_recv, sib_send, sib_recv, fw_send, fw_recv,
    w_send, w_recv, wf_sem, halo_send, halo_recv, out_sem,
):
    nvel, nsx, nsy = sizes
    nh = nvel // 2
    peers = nsx * nsy
    tile_rows, tile_cols, _ = f_hbm.shape
    depth = NVZ // nvel
    per_row = tile_cols // GROUP
    chunks = tile_rows * per_row
    share = NXY // peers
    vel = lax.axis_index("vel")
    sx = lax.axis_index("sx")
    sy = lax.axis_index("sy")
    high, low = lax.div(vel, 2), lax.rem(vel, 2)
    sibling = high * 2 + 1 - low
    me = sx * nsy + sy

    barrier = pltpu.get_barrier_semaphore()

    def greet(i, carry):
        peer = lax.rem(me + i, peers)
        pl.semaphore_signal(
            barrier, inc=1,
            device_id={"sx": lax.div(peer, nsy), "sy": lax.rem(peer, nsy)},
            device_id_type=MESH,
        )
        return carry

    for i in range(1, nh):
        pl.semaphore_signal(
            barrier, inc=1, device_id={"vel": lax.rem(high + i, nh) * 2 + low},
            device_id_type=MESH,
        )
    pl.semaphore_signal(barrier, inc=1, device_id={"vel": sibling}, device_id_type=MESH)
    lax.fori_loop(1, peers, greet, 0)

    def piece(k):
        return f_hbm.at[
            k // per_row, pl.ds(pl.multiple_of((k % per_row) * GROUP, GROUP), GROUP), :
        ]

    half_lanes = pl.ds(pl.multiple_of(low * HALF, HALF), HALF)
    sib_lanes = pl.ds(pl.multiple_of((1 - low) * HALF, HALF), HALF)

    def share_rows(owner):
        return pl.ds(pl.multiple_of(owner * share, share), share)

    def load_own(k):
        return pltpu.make_async_copy(piece(k), tiles.at[vel, k], loc_sem.at[k])

    own_weights = pltpu.make_async_copy(
        w_hbm.at[:, half_lanes], weights.at[share_rows(me), half_lanes], wloc_sem
    )
    for k in range(chunks):
        load_own(k).start()
    own_weights.start()
    pl.semaphore_wait(barrier, peers + nh - 1)

    def to_chip(k, i):
        other = lax.rem(high + i, nh)
        return pltpu.make_async_remote_copy(
            src_ref=piece(k), dst_ref=tiles.at[vel, k],
            send_sem=x_send.at[other, k], recv_sem=x_recv.at[high, k],
            device_id={"vel": other * 2 + low}, device_id_type=MESH,
        )

    def from_chip(k, i):
        other = lax.rem(high + i, nh)
        return pltpu.make_async_remote_copy(
            src_ref=piece(k), dst_ref=tiles.at[other * 2 + low, k],
            send_sem=x_send.at[other, k], recv_sem=x_recv.at[other, k],
            device_id={"vel": other * 2 + low}, device_id_type=MESH,
        )

    def to_sibling(k):
        return pltpu.make_async_remote_copy(
            src_ref=piece(k), dst_ref=tiles.at[vel, k],
            send_sem=sib_send.at[k], recv_sem=sib_recv.at[k],
            device_id={"vel": sibling}, device_id_type=MESH,
        )

    def from_sibling(k):
        return pltpu.make_async_remote_copy(
            src_ref=piece(k), dst_ref=tiles.at[sibling, k],
            send_sem=sib_send.at[k], recv_sem=sib_recv.at[k],
            device_id={"vel": sibling}, device_id_type=MESH,
        )

    def forward(k, i):
        other = lax.rem(high + i, nh)
        slot = other * 2 + low
        return pltpu.make_async_remote_copy(
            src_ref=tiles.at[slot, k], dst_ref=tiles.at[slot, k],
            send_sem=fw_send.at[other, k], recv_sem=fw_recv.at[other, k],
            device_id={"vel": sibling}, device_id_type=MESH,
        )

    def forwarded(k, i):
        other = lax.rem(high + i, nh)
        slot = other * 2 + 1 - low
        return pltpu.make_async_remote_copy(
            src_ref=tiles.at[slot, k], dst_ref=tiles.at[slot, k],
            send_sem=fw_send.at[other, k], recv_sem=fw_recv.at[other, k],
            device_id={"vel": sibling}, device_id_type=MESH,
        )

    def send_weights(i):
        peer = lax.rem(me + i, peers)
        return pltpu.make_async_remote_copy(
            src_ref=w_hbm.at[:, half_lanes], dst_ref=weights.at[share_rows(me), half_lanes],
            send_sem=w_send.at[peer], recv_sem=w_recv.at[me],
            device_id={"sx": lax.div(peer, nsy), "sy": lax.rem(peer, nsy)},
            device_id_type=MESH,
        )

    def take_weights(i):
        peer = lax.rem(me + i, peers)
        return pltpu.make_async_remote_copy(
            src_ref=w_hbm.at[:, half_lanes], dst_ref=weights.at[share_rows(peer), half_lanes],
            send_sem=w_send.at[peer], recv_sem=w_recv.at[peer],
            device_id={"sx": lax.div(peer, nsy), "sy": lax.rem(peer, nsy)},
            device_id_type=MESH,
        )

    def swap_weights(lanes):
        return pltpu.make_async_remote_copy(
            src_ref=weights.at[:, lanes], dst_ref=weights.at[:, lanes],
            send_sem=wf_sem.at[0], recv_sem=wf_sem.at[1],
            device_id={"vel": sibling}, device_id_type=MESH,
        )

    def row_halo(way):
        target = lax.rem(sx + (1 if way == 0 else nsx - 1), nsx)
        return pltpu.make_async_remote_copy(
            src_ref=row_out.at[way], dst_ref=row_in.at[way],
            send_sem=halo_send.at[way], recv_sem=halo_recv.at[way],
            device_id={"sx": target}, device_id_type=MESH,
        )

    def col_halo(way):
        target = lax.rem(sy + (1 if way == 0 else nsy - 1), nsy)
        return pltpu.make_async_remote_copy(
            src_ref=col_out.at[way], dst_ref=col_in.at[way],
            send_sem=halo_send.at[2 + way], recv_sem=halo_recv.at[2 + way],
            device_id={"sy": target}, device_id_type=MESH,
        )

    for k in range(chunks):
        for i in range(1, nh):
            to_chip(k, i).start()
        to_sibling(k).start()

    def start_weights(i, carry):
        send_weights(i).start()
        return carry

    lax.fori_loop(1, peers, start_weights, 0)

    for k in range(chunks):
        load_own(k).wait()

    for z in range(depth):
        for j in range(per_row):
            rows = slice(j * GROUP, (j + 1) * GROUP)
            lanes = slice(z * HALF, (z + 1) * HALF)
            row_out[0, rows, lanes] = tiles[
                vel, (tile_rows - 1) * per_row + j, :, z * NXY + HALF:(z + 1) * NXY
            ]
            row_out[1, rows, lanes] = tiles[vel, j, :, z * NXY:z * NXY + HALF]
    row_halo(0).start()
    row_halo(1).start()
    packed = col_out.shape[1]
    edge = depth * tile_rows * GROUP
    for way, (part, line) in enumerate(((per_row - 1, GROUP - 1), (0, 0))):
        stack = jnp.concatenate(
            [
                tiles[vel, r * per_row + part, :, z * NXY:(z + 1) * NXY]
                for r in range(tile_rows)
                for z in range(depth)
            ],
            axis=0,
        )
        pick = (
            lax.broadcasted_iota(jnp.int32, (packed, edge), 1)
            == lax.broadcasted_iota(jnp.int32, (packed, edge), 0) * GROUP + line
        )
        pick = jnp.where(pick, 1.0, 0.0).astype(BF16)
        col_out[way] = jnp.dot(pick, stack, preferred_element_type=F32).astype(BF16)
        col_halo(way).start()

    rows, cols = spread.shape
    first = vel * depth
    chosen = (
        lax.broadcasted_iota(jnp.int32, (rows, NVZ), 1)
        == (lax.broadcasted_iota(jnp.int32, (rows, NVZ), 0) >> 4) + first
    )
    fan = (
        lax.broadcasted_iota(jnp.int32, (NVZ, cols), 0)
        == lax.broadcasted_iota(jnp.int32, (NVZ, cols), 1) >> 4
    )
    own = jnp.dot(
        jnp.where(chosen, 1.0, 0.0).astype(BF16), d_ref[...], preferred_element_type=F32
    ).astype(BF16)
    wide = jnp.dot(own, jnp.where(fan, 1.0, 0.0).astype(BF16), preferred_element_type=F32)
    same = (
        lax.broadcasted_iota(jnp.int32, (rows, cols), 0) & (GROUP - 1)
    ) == (lax.broadcasted_iota(jnp.int32, (rows, cols), 1) & (GROUP - 1))
    spread[...] = jnp.where(same, wide, 0.0).astype(BF16)

    across, along = lane_speeds((NXY, 128), 0)
    column = lax.broadcasted_iota(jnp.int32, (NXY, 128), 1)
    square = across * across + along * along
    coarse = square.astype(BF16).astype(F32)
    probe = jnp.where(column == 0, 1.0, 0.0)
    probe = jnp.where(column == 1, across, probe)
    probe = jnp.where(column == 2, along, probe)
    probe = jnp.where(column == 3, coarse, probe)
    probe = jnp.where(column == 4, square - coarse, probe)
    probes[...] = probe.astype(BF16)

    vz = [(w - (NVZ - 1) / 2.0) * (8.0 / NVZ) for w in range(NVZ)]

    def relax(k):
        stack = jnp.concatenate(
            [
                tiles[v, k, :, z * NXY:(z + 1) * NXY]
                for v in range(nvel)
                for z in range(depth)
            ],
            axis=0,
        )
        sums = jnp.dot(stack, probes[...], preferred_element_type=F32)
        plain = jnp.zeros((GROUP, 128), F32)
        first_order = jnp.zeros((GROUP, 128), F32)
        second_order = jnp.zeros((GROUP, 128), F32)
        for w in range(NVZ):
            term = sums[w * GROUP:(w + 1) * GROUP]
            plain = plain + term
            first_order = first_order + vz[w] * term
            second_order = second_order + (vz[w] * vz[w]) * term

        def lanes(block, q):
            return jnp.broadcast_to(block[:, q:q + 1], (GROUP, 128))

        density = lanes(plain, 0)
        ux = lanes(plain, 1) / density
        uy = lanes(plain, 2) / density
        uz = lanes(first_order, 0) / density
        energy = lanes(plain, 3) + lanes(plain, 4) + lanes(second_order, 0)
        heat = (energy / density - (ux * ux + uy * uy + uz * uz)) / 3.0
        spread_heat = (2.0 * math.pi) * heat
        volume = (8.0 / NVX) * (8.0 / NVY) * (8.0 / NVZ)
        scale = density * volume / (spread_heat * jnp.sqrt(spread_heat))
        rate = 0.5 / heat

        def wider(block, count):
            return jnp.concatenate([block] * count, axis=1)

        vx, vy = lane_speeds((GROUP, NXY), 1)
        gap_x = vx - wider(ux, NXY // 128)
        gap_y = vy - wider(uy, NXY // 128)
        plane = jnp.exp(-(gap_x * gap_x + gap_y * gap_y) * wider(rate, NXY // 128))
        column = jnp.concatenate(
            [scale * jnp.exp(-((vz[w] - uz) * (vz[w] - uz)) * rate) for w in range(NVZ)], axis=0
        )
        head = column.astype(BF16)
        rest = (column - head.astype(F32)).astype(BF16)
        depth_mix = jnp.dot(spread[...], head, preferred_element_type=F32) + jnp.dot(
            spread[...], rest, preferred_element_type=F32
        )
        mix = jnp.dot(spread[...], stack, preferred_element_type=F32)
        even = wider(depth_mix, NXY // 128) * jnp.concatenate([plane] * depth, axis=0)
        mixed[k] = (even - mix).astype(BF16)

    vx, vy = lane_speeds((1, NXY), 1)
    pace_x, pace_y = jnp.abs(vx), jnp.abs(vy)
    toward = vy > 0.0

    def transport():
        for way in range(2):
            row_halo(way).wait_recv()
            col_halo(way).wait_recv()
        col_wide[...] = col_in[...].astype(F32)
        line = lax.broadcasted_iota(jnp.int32, (tile_cols, NXY), 0)
        for r in range(tile_rows):

            def plane_step(z, carry):
                whole = pl.ds(pl.multiple_of(z * NXY, NXY), NXY)
                left_half = pl.ds(pl.multiple_of(z * NXY, HALF), HALF)
                right_half = pl.ds(pl.multiple_of(z * NXY + HALF, HALF), HALF)
                packed_half = pl.ds(pl.multiple_of(z * HALF, HALF), HALF)

                def row(index, lanes):
                    return jnp.concatenate(
                        [tiles[vel, index * per_row + j, :, lanes] for j in range(per_row)],
                        axis=0,
                    ).astype(F32)

                current = row(r, whole)
                place = pl.ds(r * depth + z, 1)
                left = jnp.where(line == 0, col_wide[0, place, :], pltpu.roll(current, 1, 0))
                right = jnp.where(
                    line == tile_cols - 1,
                    col_wide[1, place, :],
                    pltpu.roll(current, tile_cols - 1, 0),
                )
                if r == tile_rows - 1:
                    upper = row_in[1, :, packed_half].astype(F32)
                else:
                    upper = row(r + 1, left_half)
                if r == 0:
                    lower = row_in[0, :, packed_half].astype(F32)
                else:
                    lower = row(r - 1, right_half)
                across = pace_x * (current - jnp.concatenate([upper, lower], axis=1))
                along = pace_y * (current - jnp.where(toward, left, right))
                moved = current - (
                    COURANT / (4.0 - 4.0 / NVX) * across + COURANT / (4.0 - 4.0 / NVY) * along
                )
                for j in range(per_row):
                    base[r * per_row + j, :, whole] = moved[j * GROUP:(j + 1) * GROUP]
                return carry

            lax.fori_loop(0, depth, plane_step, 0)

    def store(k):
        return pltpu.make_async_copy(
            result.at[k],
            out_hbm.at[
                k // per_row, pl.ds(pl.multiple_of((k % per_row) * GROUP, GROUP), GROUP), :
            ],
            out_sem.at[k],
        )

    def finish(k, carry):
        collision = lax.dot_general(
            mixed[k], weights[...], (((1,), (1,)), ((), ())), preferred_element_type=F32
        )
        for z in range(depth):
            lanes = slice(z * NXY, (z + 1) * NXY)
            result[k, :, lanes] = (
                base[k, :, lanes] + RELAX_RATE * collision[z * GROUP:(z + 1) * GROUP]
            ).astype(BF16)
        store(k).start()
        return carry

    gate = min(3, chunks - 1)

    def step(k, carry):
        for i in range(1, nh):
            from_chip(k, i).wait_recv()
            forward(k, i).start()
        from_sibling(k).wait_recv()
        for i in range(1, nh):
            forwarded(k, i).wait_recv()
        relax(k)

        @pl.when(k == 1)
        def _():
            own_weights.wait()

            def take(i, c):
                take_weights(i).wait_recv()
                return c

            lax.fori_loop(1, peers, take, 0)
            swap_weights(half_lanes).start()

        @pl.when(k == 2)
        def _():
            transport()

        @pl.when(k == gate)
        def _():
            swap_weights(sib_lanes).wait_recv()

        lax.fori_loop(
            jnp.where(k == gate, 0, k), jnp.where(k >= gate, k + 1, k), finish, 0
        )
        return carry

    lax.fori_loop(0, chunks, step, 0)

    for k in range(chunks):
        for i in range(1, nh):
            to_chip(k, i).wait_send()
            forward(k, i).wait_send()
        to_sibling(k).wait_send()
        store(k).wait()

    def sent(i, carry):
        send_weights(i).wait_send()
        return carry

    lax.fori_loop(1, peers, sent, 0)
    swap_weights(half_lanes).wait_send()
    for way in range(2):
        row_halo(way).wait_send()
        col_halo(way).wait_send()


def local(sizes, distribution, plane_weights, depth_weights):
    nvel, nsx, nsy = sizes
    tile_rows, tile_cols, width = distribution.shape
    depth = width // NXY
    chunks = tile_rows * tile_cols // GROUP
    packed = -(-tile_rows * depth // 16) * 16
    dma = pltpu.SemaphoreType.DMA
    cells = tile_rows * tile_cols
    return pl.pallas_call(
        functools.partial(kernel, sizes),
        out_shape=jax.ShapeDtypeStruct(distribution.shape, BF16),
        in_specs=[
            pl.BlockSpec(memory_space=pl.ANY),
            pl.BlockSpec(memory_space=pl.ANY),
            pl.BlockSpec(memory_space=pltpu.VMEM),
        ],
        out_specs=pl.BlockSpec(memory_space=pl.ANY),
        scratch_shapes=[
            pltpu.VMEM((nvel, chunks, GROUP, width), BF16),
            pltpu.VMEM((NXY, NXY), BF16),
            pltpu.VMEM((chunks, GROUP, width), F32),
            pltpu.VMEM((chunks, GROUP * depth, NXY), BF16),
            pltpu.VMEM((chunks, GROUP, width), BF16),
            pltpu.VMEM((GROUP * depth, GROUP * NVZ), BF16),
            pltpu.VMEM((NXY, 128), BF16),
            pltpu.VMEM((2, tile_cols, depth * HALF), BF16),
            pltpu.VMEM((2, tile_cols, depth * HALF), BF16),
            pltpu.VMEM((2, packed, NXY), BF16),
            pltpu.VMEM((2, packed, NXY), BF16),
            pltpu.VMEM((2, packed, NXY), F32),
            dma((chunks,)),
            dma,
            dma((nvel // 2, chunks)),
            dma((nvel // 2, chunks)),
            dma((chunks,)),
            dma((chunks,)),
            dma((nvel // 2, chunks)),
            dma((nvel // 2, chunks)),
            dma((nsx * nsy,)),
            dma((nsx * nsy,)),
            dma((2,)),
            dma((4,)),
            dma((4,)),
            dma((chunks,)),
        ],
        compiler_params=pltpu.CompilerParams(
            collective_id=0, has_side_effects=True, vmem_limit_bytes=56 * 1024 * 1024
        ),
        cost_estimate=pl.CostEstimate(
            flops=2 * cells * depth * NXY * NXY,
            bytes_accessed=4 * cells * width,
            transcendentals=cells * NXY,
        ),
    )(distribution, plane_weights, depth_weights)


def solution(mesh):
    sizes = (mesh.shape["vel"], mesh.shape["sx"], mesh.shape["sy"])
    return jax.shard_map(
        functools.partial(local, sizes),
        mesh=mesh,
        in_specs=(P("sx", "sy", "vel"), P(("sx", "sy"), None), P()),
        out_specs=P("sx", "sy", "vel"),
        check_vma=False,
    )
```

```python
import functools
import math

import jax
import jax.numpy as jnp
from jax import lax
from jax.experimental import pallas as pl
from jax.experimental.pallas import tpu as pltpu
from jax.sharding import PartitionSpec as P

NVZ = 32
NVX = 32
NVY = 32
NXY = NVX * NVY
HALF = NXY // 2
GROUP = 16
AHEAD = 2
COURANT = 0.45
RELAX_RATE = 0.3
MESH = pl.DeviceIdType.MESH
F32 = jnp.float32
BF16 = jnp.bfloat16


def lane_speeds(shape, dim):
    lane = lax.broadcasted_iota(jnp.int32, shape, dim)
    across = ((lane >> 5).astype(F32) - (NVX - 1) / 2.0) * (8.0 / NVX)
    along = ((lane & 31).astype(F32) - (NVY - 1) / 2.0) * (8.0 / NVY)
    return across, along


def kernel(
    sizes, f_hbm, w_hbm, d_ref, out_hbm,
    tiles, weights, base, mixed, result, spread, probes,
    row_out, row_in, col_out, col_in, col_wide,
    loc_sem, wloc_sem, x_send, x_recv, sib_send, sib_recv, fw_send, fw_recv,
    w_send, w_recv, wf_sem, halo_send, halo_recv, out_sem,
):
    nvel, nsx, nsy = sizes
    nh = nvel // 2
    peers = nsx * nsy
    tile_rows, tile_cols, _ = f_hbm.shape
    depth = NVZ // nvel
    per_row = tile_cols // GROUP
    chunks = tile_rows * per_row
    share = NXY // peers
    vel = lax.axis_index("vel")
    sx = lax.axis_index("sx")
    sy = lax.axis_index("sy")
    high, low = lax.div(vel, 2), lax.rem(vel, 2)
    sibling = high * 2 + 1 - low
    me = sx * nsy + sy

    barrier = pltpu.get_barrier_semaphore()

    def greet(i, carry):
        peer = lax.rem(me + i, peers)
        pl.semaphore_signal(
            barrier, inc=1,
            device_id={"sx": lax.div(peer, nsy), "sy": lax.rem(peer, nsy)},
            device_id_type=MESH,
        )
        return carry

    for i in range(1, nh):
        pl.semaphore_signal(
            barrier, inc=1, device_id={"vel": lax.rem(high + i, nh) * 2 + low},
            device_id_type=MESH,
        )
    pl.semaphore_signal(barrier, inc=1, device_id={"vel": sibling}, device_id_type=MESH)
    lax.fori_loop(1, peers, greet, 0)

    def piece(k):
        return f_hbm.at[
            k // per_row, pl.ds(pl.multiple_of((k % per_row) * GROUP, GROUP), GROUP), :
        ]

    half_lanes = pl.ds(pl.multiple_of(low * HALF, HALF), HALF)
    sib_lanes = pl.ds(pl.multiple_of((1 - low) * HALF, HALF), HALF)

    def share_rows(owner):
        return pl.ds(pl.multiple_of(owner * share, share), share)

    def load_own(k):
        return pltpu.make_async_copy(piece(k), tiles.at[vel, k], loc_sem.at[k])

    own_weights = pltpu.make_async_copy(
        w_hbm.at[:, half_lanes], weights.at[share_rows(me), half_lanes], wloc_sem
    )
    for k in range(chunks):
        load_own(k).start()
    own_weights.start()
    pl.semaphore_wait(barrier, peers + nh - 1)

    def to_chip(k, i):
        other = lax.rem(high + i, nh)
        return pltpu.make_async_remote_copy(
            src_ref=piece(k), dst_ref=tiles.at[vel, k],
            send_sem=x_send.at[other, k], recv_sem=x_recv.at[high, k],
            device_id={"vel": other * 2 + low}, device_id_type=MESH,
        )

    def from_chip(k, i):
        other = lax.rem(high + i, nh)
        return pltpu.make_async_remote_copy(
            src_ref=piece(k), dst_ref=tiles.at[other * 2 + low, k],
            send_sem=x_send.at[other, k], recv_sem=x_recv.at[other, k],
            device_id={"vel": other * 2 + low}, device_id_type=MESH,
        )

    def to_sibling(k):
        return pltpu.make_async_remote_copy(
            src_ref=piece(k), dst_ref=tiles.at[vel, k],
            send_sem=sib_send.at[k], recv_sem=sib_recv.at[k],
            device_id={"vel": sibling}, device_id_type=MESH,
        )

    def from_sibling(k):
        return pltpu.make_async_remote_copy(
            src_ref=piece(k), dst_ref=tiles.at[sibling, k],
            send_sem=sib_send.at[k], recv_sem=sib_recv.at[k],
            device_id={"vel": sibling}, device_id_type=MESH,
        )

    def forward(k, i):
        other = lax.rem(high + i, nh)
        slot = other * 2 + low
        return pltpu.make_async_remote_copy(
            src_ref=tiles.at[slot, k], dst_ref=tiles.at[slot, k],
            send_sem=fw_send.at[other, k], recv_sem=fw_recv.at[other, k],
            device_id={"vel": sibling}, device_id_type=MESH,
        )

    def forwarded(k, i):
        other = lax.rem(high + i, nh)
        slot = other * 2 + 1 - low
        return pltpu.make_async_remote_copy(
            src_ref=tiles.at[slot, k], dst_ref=tiles.at[slot, k],
            send_sem=fw_send.at[other, k], recv_sem=fw_recv.at[other, k],
            device_id={"vel": sibling}, device_id_type=MESH,
        )

    def send_weights(i):
        peer = lax.rem(me + i, peers)
        return pltpu.make_async_remote_copy(
            src_ref=w_hbm.at[:, half_lanes], dst_ref=weights.at[share_rows(me), half_lanes],
            send_sem=w_send.at[peer], recv_sem=w_recv.at[me],
            device_id={"sx": lax.div(peer, nsy), "sy": lax.rem(peer, nsy)},
            device_id_type=MESH,
        )

    def take_weights(i):
        peer = lax.rem(me + i, peers)
        return pltpu.make_async_remote_copy(
            src_ref=w_hbm.at[:, half_lanes], dst_ref=weights.at[share_rows(peer), half_lanes],
            send_sem=w_send.at[peer], recv_sem=w_recv.at[peer],
            device_id={"sx": lax.div(peer, nsy), "sy": lax.rem(peer, nsy)},
            device_id_type=MESH,
        )

    def swap_weights(lanes):
        return pltpu.make_async_remote_copy(
            src_ref=weights.at[:, lanes], dst_ref=weights.at[:, lanes],
            send_sem=wf_sem.at[0], recv_sem=wf_sem.at[1],
            device_id={"vel": sibling}, device_id_type=MESH,
        )

    def row_halo(way):
        target = lax.rem(sx + (1 if way == 0 else nsx - 1), nsx)
        return pltpu.make_async_remote_copy(
            src_ref=row_out.at[way], dst_ref=row_in.at[way],
            send_sem=halo_send.at[way], recv_sem=halo_recv.at[way],
            device_id={"sx": target}, device_id_type=MESH,
        )

    def col_halo(way):
        target = lax.rem(sy + (1 if way == 0 else nsy - 1), nsy)
        return pltpu.make_async_remote_copy(
            src_ref=col_out.at[way], dst_ref=col_in.at[way],
            send_sem=halo_send.at[2 + way], recv_sem=halo_recv.at[2 + way],
            device_id={"sy": target}, device_id_type=MESH,
        )

    def launch(k):
        for i in range(1, nh):
            to_chip(k, i).start()
        to_sibling(k).start()

    for k in range(min(AHEAD, chunks)):
        launch(k)

    def start_weights(i, carry):
        send_weights(i).start()
        return carry

    lax.fori_loop(1, peers, start_weights, 0)

    for k in range(chunks):
        load_own(k).wait()

    for z in range(depth):
        for j in range(per_row):
            rows = slice(j * GROUP, (j + 1) * GROUP)
            lanes = slice(z * HALF, (z + 1) * HALF)
            row_out[0, rows, lanes] = tiles[
                vel, (tile_rows - 1) * per_row + j, :, z * NXY + HALF:(z + 1) * NXY
            ]
            row_out[1, rows, lanes] = tiles[vel, j, :, z * NXY:z * NXY + HALF]
    row_halo(0).start()
    row_halo(1).start()
    packed = col_out.shape[1]
    edge = depth * tile_rows * GROUP
    for way, (part, line) in enumerate(((per_row - 1, GROUP - 1), (0, 0))):
        stack = jnp.concatenate(
            [
                tiles[vel, r * per_row + part, :, z * NXY:(z + 1) * NXY]
                for r in range(tile_rows)
                for z in range(depth)
            ],
            axis=0,
        )
        pick = (
            lax.broadcasted_iota(jnp.int32, (packed, edge), 1)
            == lax.broadcasted_iota(jnp.int32, (packed, edge), 0) * GROUP + line
        )
        pick = jnp.where(pick, 1.0, 0.0).astype(BF16)
        col_out[way] = jnp.dot(pick, stack, preferred_element_type=F32).astype(BF16)
        col_halo(way).start()

    rows, cols = spread.shape
    first = vel * depth
    chosen = (
        lax.broadcasted_iota(jnp.int32, (rows, NVZ), 1)
        == (lax.broadcasted_iota(jnp.int32, (rows, NVZ), 0) >> 4) + first
    )
    fan = (
        lax.broadcasted_iota(jnp.int32, (NVZ, cols), 0)
        == lax.broadcasted_iota(jnp.int32, (NVZ, cols), 1) >> 4
    )
    own = jnp.dot(
        jnp.where(chosen, 1.0, 0.0).astype(BF16), d_ref[...], preferred_element_type=F32
    ).astype(BF16)
    wide = jnp.dot(own, jnp.where(fan, 1.0, 0.0).astype(BF16), preferred_element_type=F32)
    same = (
        lax.broadcasted_iota(jnp.int32, (rows, cols), 0) & (GROUP - 1)
    ) == (lax.broadcasted_iota(jnp.int32, (rows, cols), 1) & (GROUP - 1))
    spread[...] = jnp.where(same, wide, 0.0).astype(BF16)

    across, along = lane_speeds((NXY, 128), 0)
    column = lax.broadcasted_iota(jnp.int32, (NXY, 128), 1)
    square = across * across + along * along
    coarse = square.astype(BF16).astype(F32)
    probe = jnp.where(column == 0, 1.0, 0.0)
    probe = jnp.where(column == 1, across, probe)
    probe = jnp.where(column == 2, along, probe)
    probe = jnp.where(column == 3, coarse, probe)
    probe = jnp.where(column == 4, square - coarse, probe)
    probes[...] = probe.astype(BF16)

    vz = [(w - (NVZ - 1) / 2.0) * (8.0 / NVZ) for w in range(NVZ)]

    def relax(k):
        stack = jnp.concatenate(
            [
                tiles[v, k, :, z * NXY:(z + 1) * NXY]
                for v in range(nvel)
                for z in range(depth)
            ],
            axis=0,
        )
        sums = jnp.dot(stack, probes[...], preferred_element_type=F32)
        plain = jnp.zeros((GROUP, 128), F32)
        first_order = jnp.zeros((GROUP, 128), F32)
        second_order = jnp.zeros((GROUP, 128), F32)
        for w in range(NVZ):
            term = sums[w * GROUP:(w + 1) * GROUP]
            plain = plain + term
            first_order = first_order + vz[w] * term
            second_order = second_order + (vz[w] * vz[w]) * term

        def lanes(block, q):
            return jnp.broadcast_to(block[:, q:q + 1], (GROUP, 128))

        density = lanes(plain, 0)
        ux = lanes(plain, 1) / density
        uy = lanes(plain, 2) / density
        uz = lanes(first_order, 0) / density
        energy = lanes(plain, 3) + lanes(plain, 4) + lanes(second_order, 0)
        heat = (energy / density - (ux * ux + uy * uy + uz * uz)) / 3.0
        spread_heat = (2.0 * math.pi) * heat
        volume = (8.0 / NVX) * (8.0 / NVY) * (8.0 / NVZ)
        scale = density * volume / (spread_heat * jnp.sqrt(spread_heat))
        rate = 0.5 / heat

        def wider(block, count):
            return jnp.concatenate([block] * count, axis=1)

        vx, vy = lane_speeds((GROUP, NXY), 1)
        gap_x = vx - wider(ux, NXY // 128)
        gap_y = vy - wider(uy, NXY // 128)
        plane = jnp.exp(-(gap_x * gap_x + gap_y * gap_y) * wider(rate, NXY // 128))
        column = jnp.concatenate(
            [scale * jnp.exp(-((vz[w] - uz) * (vz[w] - uz)) * rate) for w in range(NVZ)], axis=0
        )
        head = column.astype(BF16)
        rest = (column - head.astype(F32)).astype(BF16)
        depth_mix = jnp.dot(spread[...], head, preferred_element_type=F32) + jnp.dot(
            spread[...], rest, preferred_element_type=F32
        )
        mix = jnp.dot(spread[...], stack, preferred_element_type=F32)
        even = wider(depth_mix, NXY // 128) * jnp.concatenate([plane] * depth, axis=0)
        mixed[k] = (even - mix).astype(BF16)

    vx, vy = lane_speeds((1, NXY), 1)
    pace_x, pace_y = jnp.abs(vx), jnp.abs(vy)
    toward = vy > 0.0

    def transport():
        for way in range(2):
            row_halo(way).wait_recv()
            col_halo(way).wait_recv()
        col_wide[...] = col_in[...].astype(F32)
        line = lax.broadcasted_iota(jnp.int32, (tile_cols, NXY), 0)
        for r in range(tile_rows):

            def plane_step(z, carry):
                whole = pl.ds(pl.multiple_of(z * NXY, NXY), NXY)
                left_half = pl.ds(pl.multiple_of(z * NXY, HALF), HALF)
                right_half = pl.ds(pl.multiple_of(z * NXY + HALF, HALF), HALF)
                packed_half = pl.ds(pl.multiple_of(z * HALF, HALF), HALF)

                def row(index, lanes):
                    return jnp.concatenate(
                        [tiles[vel, index * per_row + j, :, lanes] for j in range(per_row)],
                        axis=0,
                    ).astype(F32)

                current = row(r, whole)
                place = pl.ds(r * depth + z, 1)
                left = jnp.where(line == 0, col_wide[0, place, :], pltpu.roll(current, 1, 0))
                right = jnp.where(
                    line == tile_cols - 1,
                    col_wide[1, place, :],
                    pltpu.roll(current, tile_cols - 1, 0),
                )
                if r == tile_rows - 1:
                    upper = row_in[1, :, packed_half].astype(F32)
                else:
                    upper = row(r + 1, left_half)
                if r == 0:
                    lower = row_in[0, :, packed_half].astype(F32)
                else:
                    lower = row(r - 1, right_half)
                across = pace_x * (current - jnp.concatenate([upper, lower], axis=1))
                along = pace_y * (current - jnp.where(toward, left, right))
                moved = current - (
                    COURANT / (4.0 - 4.0 / NVX) * across + COURANT / (4.0 - 4.0 / NVY) * along
                )
                for j in range(per_row):
                    base[r * per_row + j, :, whole] = moved[j * GROUP:(j + 1) * GROUP]
                return carry

            lax.fori_loop(0, depth, plane_step, 0)

    def store(k):
        return pltpu.make_async_copy(
            result.at[k],
            out_hbm.at[
                k // per_row, pl.ds(pl.multiple_of((k % per_row) * GROUP, GROUP), GROUP), :
            ],
            out_sem.at[k],
        )

    def finish(k, carry):
        collision = lax.dot_general(
            mixed[k], weights[...], (((1,), (1,)), ((), ())), preferred_element_type=F32
        )
        for z in range(depth):
            lanes = slice(z * NXY, (z + 1) * NXY)
            result[k, :, lanes] = (
                base[k, :, lanes] + RELAX_RATE * collision[z * GROUP:(z + 1) * GROUP]
            ).astype(BF16)
        store(k).start()
        return carry

    gate = min(3, chunks - 1)

    def step(k, carry):
        for i in range(1, nh):
            to_chip(k, i).wait_send()

        @pl.when(k + AHEAD < chunks)
        def _():
            launch(k + AHEAD)

        for i in range(1, nh):
            from_chip(k, i).wait_recv()
            forward(k, i).start()
        from_sibling(k).wait_recv()
        for i in range(1, nh):
            forwarded(k, i).wait_recv()
        relax(k)

        @pl.when(k == 1)
        def _():
            own_weights.wait()

            def take(i, c):
                take_weights(i).wait_recv()
                return c

            lax.fori_loop(1, peers, take, 0)
            swap_weights(half_lanes).start()

        @pl.when(k == 2)
        def _():
            transport()

        @pl.when(k == gate)
        def _():
            swap_weights(sib_lanes).wait_recv()

        lax.fori_loop(
            jnp.where(k == gate, 0, k), jnp.where(k >= gate, k + 1, k), finish, 0
        )
        return carry

    lax.fori_loop(0, chunks, step, 0)

    for k in range(chunks):
        for i in range(1, nh):
            forward(k, i).wait_send()
        to_sibling(k).wait_send()
        store(k).wait()

    def sent(i, carry):
        send_weights(i).wait_send()
        return carry

    lax.fori_loop(1, peers, sent, 0)
    swap_weights(half_lanes).wait_send()
    for way in range(2):
        row_halo(way).wait_send()
        col_halo(way).wait_send()


def local(sizes, distribution, plane_weights, depth_weights):
    nvel, nsx, nsy = sizes
    tile_rows, tile_cols, width = distribution.shape
    depth = width // NXY
    chunks = tile_rows * tile_cols // GROUP
    packed = -(-tile_rows * depth // 16) * 16
    dma = pltpu.SemaphoreType.DMA
    cells = tile_rows * tile_cols
    return pl.pallas_call(
        functools.partial(kernel, sizes),
        out_shape=jax.ShapeDtypeStruct(distribution.shape, BF16),
        in_specs=[
            pl.BlockSpec(memory_space=pl.ANY),
            pl.BlockSpec(memory_space=pl.ANY),
            pl.BlockSpec(memory_space=pltpu.VMEM),
        ],
        out_specs=pl.BlockSpec(memory_space=pl.ANY),
        scratch_shapes=[
            pltpu.VMEM((nvel, chunks, GROUP, width), BF16),
            pltpu.VMEM((NXY, NXY), BF16),
            pltpu.VMEM((chunks, GROUP, width), F32),
            pltpu.VMEM((chunks, GROUP * depth, NXY), BF16),
            pltpu.VMEM((chunks, GROUP, width), BF16),
            pltpu.VMEM((GROUP * depth, GROUP * NVZ), BF16),
            pltpu.VMEM((NXY, 128), BF16),
            pltpu.VMEM((2, tile_cols, depth * HALF), BF16),
            pltpu.VMEM((2, tile_cols, depth * HALF), BF16),
            pltpu.VMEM((2, packed, NXY), BF16),
            pltpu.VMEM((2, packed, NXY), BF16),
            pltpu.VMEM((2, packed, NXY), F32),
            dma((chunks,)),
            dma,
            dma((nvel // 2, chunks)),
            dma((nvel // 2, chunks)),
            dma((chunks,)),
            dma((chunks,)),
            dma((nvel // 2, chunks)),
            dma((nvel // 2, chunks)),
            dma((nsx * nsy,)),
            dma((nsx * nsy,)),
            dma((2,)),
            dma((4,)),
            dma((4,)),
            dma((chunks,)),
        ],
        compiler_params=pltpu.CompilerParams(
            collective_id=0, has_side_effects=True, vmem_limit_bytes=56 * 1024 * 1024
        ),
        cost_estimate=pl.CostEstimate(
            flops=2 * cells * depth * NXY * NXY,
            bytes_accessed=4 * cells * width,
            transcendentals=cells * NXY,
        ),
    )(distribution, plane_weights, depth_weights)


def solution(mesh):
    sizes = (mesh.shape["vel"], mesh.shape["sx"], mesh.shape["sy"])
    return jax.shard_map(
        functools.partial(local, sizes),
        mesh=mesh,
        in_specs=(P("sx", "sy", "vel"), P(("sx", "sy"), None), P()),
        out_specs=P("sx", "sy", "vel"),
        check_vma=False,
    )
```

```python
import functools
import math

import jax
import jax.numpy as jnp
from jax import lax
from jax.experimental import pallas as pl
from jax.experimental.pallas import tpu as pltpu
from jax.sharding import PartitionSpec as P

NVZ = 32
NVX = 32
NVY = 32
NXY = NVX * NVY
HALF = NXY // 2
GROUP = 16
COURANT = 0.45
RELAX_RATE = 0.3
MESH = pl.DeviceIdType.MESH
F32 = jnp.float32
BF16 = jnp.bfloat16


def lane_speeds(shape, dim):
    lane = lax.broadcasted_iota(jnp.int32, shape, dim)
    across = ((lane >> 5).astype(F32) - (NVX - 1) / 2.0) * (8.0 / NVX)
    along = ((lane & 31).astype(F32) - (NVY - 1) / 2.0) * (8.0 / NVY)
    return across, along


def kernel(
    sizes, f_hbm, w_hbm, d_ref, out_hbm,
    tiles, weights, base, mixed, result, spread, probes,
    row_out, row_in, col_out, col_in, col_wide,
    loc_sem, wloc_sem, x_send, x_recv, sib_send, sib_recv, fw_send, fw_recv,
    w_send, w_recv, wf_sem, halo_send, halo_recv, out_sem,
):
    nvel, nsx, nsy = sizes
    nh = nvel // 2
    peers = nsx * nsy
    tile_rows, tile_cols, _ = f_hbm.shape
    depth = NVZ // nvel
    per_row = tile_cols // GROUP
    chunks = tile_rows * per_row
    share = NXY // peers
    vel = lax.axis_index("vel")
    sx = lax.axis_index("sx")
    sy = lax.axis_index("sy")
    high, low = lax.div(vel, 2), lax.rem(vel, 2)
    sibling = high * 2 + 1 - low
    me = sx * nsy + sy

    barrier = pltpu.get_barrier_semaphore()

    def greet(i, carry):
        peer = lax.rem(me + i, peers)
        pl.semaphore_signal(
            barrier, inc=1,
            device_id={"sx": lax.div(peer, nsy), "sy": lax.rem(peer, nsy)},
            device_id_type=MESH,
        )
        return carry

    for i in range(1, nh):
        pl.semaphore_signal(
            barrier, inc=1, device_id={"vel": lax.rem(high + i, nh) * 2 + low},
            device_id_type=MESH,
        )
    pl.semaphore_signal(barrier, inc=1, device_id={"vel": sibling}, device_id_type=MESH)
    lax.fori_loop(1, peers, greet, 0)

    def piece(k):
        return f_hbm.at[
            k // per_row, pl.ds(pl.multiple_of((k % per_row) * GROUP, GROUP), GROUP), :
        ]

    half_lanes = pl.ds(pl.multiple_of(low * HALF, HALF), HALF)
    sib_lanes = pl.ds(pl.multiple_of((1 - low) * HALF, HALF), HALF)

    def share_rows(owner):
        return pl.ds(pl.multiple_of(owner * share, share), share)

    def load_own(k):
        return pltpu.make_async_copy(piece(k), tiles.at[vel, k], loc_sem.at[k])

    own_weights = pltpu.make_async_copy(
        w_hbm.at[:, half_lanes], weights.at[share_rows(me), half_lanes], wloc_sem
    )
    for k in range(chunks):
        load_own(k).start()
    own_weights.start()
    pl.semaphore_wait(barrier, peers + nh - 1)

    def to_chip(k, i):
        other = lax.rem(high + i, nh)
        return pltpu.make_async_remote_copy(
            src_ref=piece(k), dst_ref=tiles.at[vel, k],
            send_sem=x_send.at[other, k], recv_sem=x_recv.at[high, k],
            device_id={"vel": other * 2 + low}, device_id_type=MESH,
        )

    def from_chip(k, i):
        other = lax.rem(high + i, nh)
        return pltpu.make_async_remote_copy(
            src_ref=piece(k), dst_ref=tiles.at[other * 2 + low, k],
            send_sem=x_send.at[other, k], recv_sem=x_recv.at[other, k],
            device_id={"vel": other * 2 + low}, device_id_type=MESH,
        )

    def to_sibling(k):
        return pltpu.make_async_remote_copy(
            src_ref=piece(k), dst_ref=tiles.at[vel, k],
            send_sem=sib_send.at[k], recv_sem=sib_recv.at[k],
            device_id={"vel": sibling}, device_id_type=MESH,
        )

    def from_sibling(k):
        return pltpu.make_async_remote_copy(
            src_ref=piece(k), dst_ref=tiles.at[sibling, k],
            send_sem=sib_send.at[k], recv_sem=sib_recv.at[k],
            device_id={"vel": sibling}, device_id_type=MESH,
        )

    def forward(k, i):
        other = lax.rem(high + i, nh)
        slot = other * 2 + low
        return pltpu.make_async_remote_copy(
            src_ref=tiles.at[slot, k], dst_ref=tiles.at[slot, k],
            send_sem=fw_send.at[other, k], recv_sem=fw_recv.at[other, k],
            device_id={"vel": sibling}, device_id_type=MESH,
        )

    def forwarded(k, i):
        other = lax.rem(high + i, nh)
        slot = other * 2 + 1 - low
        return pltpu.make_async_remote_copy(
            src_ref=tiles.at[slot, k], dst_ref=tiles.at[slot, k],
            send_sem=fw_send.at[other, k], recv_sem=fw_recv.at[other, k],
            device_id={"vel": sibling}, device_id_type=MESH,
        )

    def send_weights(i):
        peer = lax.rem(me + i, peers)
        return pltpu.make_async_remote_copy(
            src_ref=w_hbm.at[:, half_lanes], dst_ref=weights.at[share_rows(me), half_lanes],
            send_sem=w_send.at[peer], recv_sem=w_recv.at[me],
            device_id={"sx": lax.div(peer, nsy), "sy": lax.rem(peer, nsy)},
            device_id_type=MESH,
        )

    def take_weights(i):
        peer = lax.rem(me + i, peers)
        return pltpu.make_async_remote_copy(
            src_ref=w_hbm.at[:, half_lanes], dst_ref=weights.at[share_rows(peer), half_lanes],
            send_sem=w_send.at[peer], recv_sem=w_recv.at[peer],
            device_id={"sx": lax.div(peer, nsy), "sy": lax.rem(peer, nsy)},
            device_id_type=MESH,
        )

    def swap_weights(lanes):
        return pltpu.make_async_remote_copy(
            src_ref=weights.at[:, lanes], dst_ref=weights.at[:, lanes],
            send_sem=wf_sem.at[0], recv_sem=wf_sem.at[1],
            device_id={"vel": sibling}, device_id_type=MESH,
        )

    def row_halo(way):
        target = lax.rem(sx + (1 if way == 0 else nsx - 1), nsx)
        return pltpu.make_async_remote_copy(
            src_ref=row_out.at[way], dst_ref=row_in.at[way],
            send_sem=halo_send.at[way], recv_sem=halo_recv.at[way],
            device_id={"sx": target}, device_id_type=MESH,
        )

    def col_halo(way):
        target = lax.rem(sy + (1 if way == 0 else nsy - 1), nsy)
        return pltpu.make_async_remote_copy(
            src_ref=col_out.at[way], dst_ref=col_in.at[way],
            send_sem=halo_send.at[2 + way], recv_sem=halo_recv.at[2 + way],
            device_id={"sy": target}, device_id_type=MESH,
        )

    for k in range(chunks):
        for i in range(1, nh):
            to_chip(k, i).start()
        to_sibling(k).start()

    def start_weights(i, carry):
        send_weights(i).start()
        return carry

    lax.fori_loop(1, peers, start_weights, 0)

    for k in range(chunks):
        load_own(k).wait()

    for z in range(depth):
        for j in range(per_row):
            rows = slice(j * GROUP, (j + 1) * GROUP)
            lanes = slice(z * HALF, (z + 1) * HALF)
            row_out[0, rows, lanes] = tiles[
                vel, (tile_rows - 1) * per_row + j, :, z * NXY + HALF:(z + 1) * NXY
            ]
            row_out[1, rows, lanes] = tiles[vel, j, :, z * NXY:z * NXY + HALF]
    row_halo(0).start()
    row_halo(1).start()
    packed = col_out.shape[1]
    edge = depth * tile_rows * GROUP
    for way, (part, line) in enumerate(((per_row - 1, GROUP - 1), (0, 0))):
        stack = jnp.concatenate(
            [
                tiles[vel, r * per_row + part, :, z * NXY:(z + 1) * NXY]
                for r in range(tile_rows)
                for z in range(depth)
            ],
            axis=0,
        )
        pick = (
            lax.broadcasted_iota(jnp.int32, (packed, edge), 1)
            == lax.broadcasted_iota(jnp.int32, (packed, edge), 0) * GROUP + line
        )
        pick = jnp.where(pick, 1.0, 0.0).astype(BF16)
        col_out[way] = jnp.dot(pick, stack, preferred_element_type=F32).astype(BF16)
        col_halo(way).start()

    rows, cols = spread.shape
    first = vel * depth
    chosen = (
        lax.broadcasted_iota(jnp.int32, (rows, NVZ), 1)
        == (lax.broadcasted_iota(jnp.int32, (rows, NVZ), 0) >> 4) + first
    )
    fan = (
        lax.broadcasted_iota(jnp.int32, (NVZ, cols), 0)
        == lax.broadcasted_iota(jnp.int32, (NVZ, cols), 1) >> 4
    )
    own = jnp.dot(
        jnp.where(chosen, 1.0, 0.0).astype(BF16), d_ref[...], preferred_element_type=F32
    ).astype(BF16)
    wide = jnp.dot(own, jnp.where(fan, 1.0, 0.0).astype(BF16), preferred_element_type=F32)
    same = (
        lax.broadcasted_iota(jnp.int32, (rows, cols), 0) & (GROUP - 1)
    ) == (lax.broadcasted_iota(jnp.int32, (rows, cols), 1) & (GROUP - 1))
    spread[...] = jnp.where(same, wide, 0.0).astype(BF16)

    across, along = lane_speeds((NXY, 128), 0)
    column = lax.broadcasted_iota(jnp.int32, (NXY, 128), 1)
    square = across * across + along * along
    coarse = square.astype(BF16).astype(F32)
    probe = jnp.where(column == 0, 1.0, 0.0)
    probe = jnp.where(column == 1, across, probe)
    probe = jnp.where(column == 2, along, probe)
    probe = jnp.where(column == 3, coarse, probe)
    probe = jnp.where(column == 4, square - coarse, probe)
    probes[...] = probe.astype(BF16)

    vz = [(w - (NVZ - 1) / 2.0) * (8.0 / NVZ) for w in range(NVZ)]

    def relax(k):
        stack = jnp.concatenate(
            [
                tiles[v, k, :, z * NXY:(z + 1) * NXY]
                for v in range(nvel)
                for z in range(depth)
            ],
            axis=0,
        )
        sums = jnp.dot(stack, probes[...], preferred_element_type=F32)
        plain = jnp.zeros((GROUP, 128), F32)
        first_order = jnp.zeros((GROUP, 128), F32)
        second_order = jnp.zeros((GROUP, 128), F32)
        for w in range(NVZ):
            term = sums[w * GROUP:(w + 1) * GROUP]
            plain = plain + term
            first_order = first_order + vz[w] * term
            second_order = second_order + (vz[w] * vz[w]) * term

        def lanes(block, q):
            return jnp.broadcast_to(block[:, q:q + 1], (GROUP, 128))

        density = lanes(plain, 0)
        ux = lanes(plain, 1) / density
        uy = lanes(plain, 2) / density
        uz = lanes(first_order, 0) / density
        energy = lanes(plain, 3) + lanes(plain, 4) + lanes(second_order, 0)
        heat = (energy / density - (ux * ux + uy * uy + uz * uz)) / 3.0
        spread_heat = (2.0 * math.pi) * heat
        volume = (8.0 / NVX) * (8.0 / NVY) * (8.0 / NVZ)
        scale = density * volume / (spread_heat * jnp.sqrt(spread_heat))
        rate = 0.5 / heat

        def wider(block, count):
            return jnp.concatenate([block] * count, axis=1)

        vx, vy = lane_speeds((GROUP, NXY), 1)
        gap_x = vx - wider(ux, NXY // 128)
        gap_y = vy - wider(uy, NXY // 128)
        plane = jnp.exp(-(gap_x * gap_x + gap_y * gap_y) * wider(rate, NXY // 128))
        column = jnp.concatenate(
            [scale * jnp.exp(-((vz[w] - uz) * (vz[w] - uz)) * rate) for w in range(NVZ)], axis=0
        )
        head = column.astype(BF16)
        rest = (column - head.astype(F32)).astype(BF16)
        depth_mix = jnp.dot(spread[...], head, preferred_element_type=F32) + jnp.dot(
            spread[...], rest, preferred_element_type=F32
        )
        mix = jnp.dot(spread[...], stack, preferred_element_type=F32)
        even = wider(depth_mix, NXY // 128) * jnp.concatenate([plane] * depth, axis=0)
        mixed[k] = (even - mix).astype(BF16)

    vx, vy = lane_speeds((1, NXY), 1)
    pace_x, pace_y = jnp.abs(vx), jnp.abs(vy)
    toward = vy > 0.0

    def transport():
        for way in range(2):
            row_halo(way).wait_recv()
            col_halo(way).wait_recv()
        col_wide[...] = col_in[...].astype(F32)
        line = lax.broadcasted_iota(jnp.int32, (tile_cols, NXY), 0)
        for r in range(tile_rows):

            def plane_step(z, carry):
                whole = pl.ds(pl.multiple_of(z * NXY, NXY), NXY)
                left_half = pl.ds(pl.multiple_of(z * NXY, HALF), HALF)
                right_half = pl.ds(pl.multiple_of(z * NXY + HALF, HALF), HALF)
                packed_half = pl.ds(pl.multiple_of(z * HALF, HALF), HALF)

                def row(index, lanes):
                    return jnp.concatenate(
                        [tiles[vel, index * per_row + j, :, lanes] for j in range(per_row)],
                        axis=0,
                    ).astype(F32)

                current = row(r, whole)
                place = pl.ds(r * depth + z, 1)
                left = jnp.where(line == 0, col_wide[0, place, :], pltpu.roll(current, 1, 0))
                right = jnp.where(
                    line == tile_cols - 1,
                    col_wide[1, place, :],
                    pltpu.roll(current, tile_cols - 1, 0),
                )
                if r == tile_rows - 1:
                    upper = row_in[1, :, packed_half].astype(F32)
                else:
                    upper = row(r + 1, left_half)
                if r == 0:
                    lower = row_in[0, :, packed_half].astype(F32)
                else:
                    lower = row(r - 1, right_half)
                across = pace_x * (current - jnp.concatenate([upper, lower], axis=1))
                along = pace_y * (current - jnp.where(toward, left, right))
                moved = current - (
                    COURANT / (4.0 - 4.0 / NVX) * across + COURANT / (4.0 - 4.0 / NVY) * along
                )
                for j in range(per_row):
                    base[r * per_row + j, :, whole] = moved[j * GROUP:(j + 1) * GROUP]
                return carry

            lax.fori_loop(0, depth, plane_step, 0)

    def store(k):
        return pltpu.make_async_copy(
            result.at[k],
            out_hbm.at[
                k // per_row, pl.ds(pl.multiple_of((k % per_row) * GROUP, GROUP), GROUP), :
            ],
            out_sem.at[k],
        )

    def finish(k, carry):
        collision = lax.dot_general(
            mixed[k], weights[...], (((1,), (1,)), ((), ())), preferred_element_type=F32
        )
        for z in range(depth):
            lanes = slice(z * NXY, (z + 1) * NXY)
            result[k, :, lanes] = (
                base[k, :, lanes] + RELAX_RATE * collision[z * GROUP:(z + 1) * GROUP]
            ).astype(BF16)
        store(k).start()
        return carry

    gate = chunks - 1

    def step(k, carry):
        for i in range(1, nh):
            from_chip(k, i).wait_recv()
            forward(k, i).start()
        from_sibling(k).wait_recv()
        for i in range(1, nh):
            forwarded(k, i).wait_recv()
        relax(k)

        @pl.when(k == chunks - 2)
        def _():
            own_weights.wait()

            def take(i, c):
                take_weights(i).wait_recv()
                return c

            lax.fori_loop(1, peers, take, 0)
            swap_weights(half_lanes).start()

        @pl.when(k == 2)
        def _():
            transport()

        @pl.when(k == gate)
        def _():
            swap_weights(sib_lanes).wait_recv()

        lax.fori_loop(
            jnp.where(k == gate, 0, k), jnp.where(k >= gate, k + 1, k), finish, 0
        )
        return carry

    lax.fori_loop(0, chunks, step, 0)

    for k in range(chunks):
        for i in range(1, nh):
            to_chip(k, i).wait_send()
            forward(k, i).wait_send()
        to_sibling(k).wait_send()
        store(k).wait()

    def sent(i, carry):
        send_weights(i).wait_send()
        return carry

    lax.fori_loop(1, peers, sent, 0)
    swap_weights(half_lanes).wait_send()
    for way in range(2):
        row_halo(way).wait_send()
        col_halo(way).wait_send()


def local(sizes, distribution, plane_weights, depth_weights):
    nvel, nsx, nsy = sizes
    tile_rows, tile_cols, width = distribution.shape
    depth = width // NXY
    chunks = tile_rows * tile_cols // GROUP
    packed = -(-tile_rows * depth // 16) * 16
    dma = pltpu.SemaphoreType.DMA
    cells = tile_rows * tile_cols
    return pl.pallas_call(
        functools.partial(kernel, sizes),
        out_shape=jax.ShapeDtypeStruct(distribution.shape, BF16),
        in_specs=[
            pl.BlockSpec(memory_space=pl.ANY),
            pl.BlockSpec(memory_space=pl.ANY),
            pl.BlockSpec(memory_space=pltpu.VMEM),
        ],
        out_specs=pl.BlockSpec(memory_space=pl.ANY),
        scratch_shapes=[
            pltpu.VMEM((nvel, chunks, GROUP, width), BF16),
            pltpu.VMEM((NXY, NXY), BF16),
            pltpu.VMEM((chunks, GROUP, width), F32),
            pltpu.VMEM((chunks, GROUP * depth, NXY), BF16),
            pltpu.VMEM((chunks, GROUP, width), BF16),
            pltpu.VMEM((GROUP * depth, GROUP * NVZ), BF16),
            pltpu.VMEM((NXY, 128), BF16),
            pltpu.VMEM((2, tile_cols, depth * HALF), BF16),
            pltpu.VMEM((2, tile_cols, depth * HALF), BF16),
            pltpu.VMEM((2, packed, NXY), BF16),
            pltpu.VMEM((2, packed, NXY), BF16),
            pltpu.VMEM((2, packed, NXY), F32),
            dma((chunks,)),
            dma,
            dma((nvel // 2, chunks)),
            dma((nvel // 2, chunks)),
            dma((chunks,)),
            dma((chunks,)),
            dma((nvel // 2, chunks)),
            dma((nvel // 2, chunks)),
            dma((nsx * nsy,)),
            dma((nsx * nsy,)),
            dma((2,)),
            dma((4,)),
            dma((4,)),
            dma((chunks,)),
        ],
        compiler_params=pltpu.CompilerParams(
            collective_id=0, has_side_effects=True, vmem_limit_bytes=56 * 1024 * 1024
        ),
        cost_estimate=pl.CostEstimate(
            flops=2 * cells * depth * NXY * NXY,
            bytes_accessed=4 * cells * width,
            transcendentals=cells * NXY,
        ),
    )(distribution, plane_weights, depth_weights)


def solution(mesh):
    sizes = (mesh.shape["vel"], mesh.shape["sx"], mesh.shape["sy"])
    return jax.shard_map(
        functools.partial(local, sizes),
        mesh=mesh,
        in_specs=(P("sx", "sy", "vel"), P(("sx", "sy"), None), P()),
        out_specs=P("sx", "sy", "vel"),
        check_vma=False,
    )
```

```python
import functools
import math

import jax
import jax.numpy as jnp
from jax import lax
from jax.experimental import pallas as pl
from jax.experimental.pallas import tpu as pltpu
from jax.sharding import PartitionSpec as P

NVZ = 32
NVX = 32
NVY = 32
NXY = NVX * NVY
HALF = NXY // 2
GROUP = 16
COURANT = 0.45
RELAX_RATE = 0.3
MESH = pl.DeviceIdType.MESH
F32 = jnp.float32
BF16 = jnp.bfloat16


def lane_speeds(shape, dim):
    lane = lax.broadcasted_iota(jnp.int32, shape, dim)
    across = ((lane >> 5).astype(F32) - (NVX - 1) / 2.0) * (8.0 / NVX)
    along = ((lane & 31).astype(F32) - (NVY - 1) / 2.0) * (8.0 / NVY)
    return across, along


def kernel(
    sizes, f_hbm, w_hbm, d_ref, out_hbm,
    own, tiles, weights, base, mixed, result, spread, probes, near_mix, near_sums,
    back_out, back_in,
    row_out, row_in, col_out, col_in, col_wide,
    loc_sem, part_sem, wloc_sem, x_send, x_recv, back_send, back_recv,
    w_send, w_recv, wf_sem, halo_send, halo_recv, out_sem,
):
    nvel, nsx, nsy = sizes
    nh = nvel // 2
    peers = nsx * nsy
    tile_rows, tile_cols, _ = f_hbm.shape
    depth = NVZ // nvel
    per_row = tile_cols // GROUP
    chunks = tile_rows * per_row
    share = NXY // peers
    vel = lax.axis_index("vel")
    sx = lax.axis_index("sx")
    sy = lax.axis_index("sy")
    high, low = lax.div(vel, 2), lax.rem(vel, 2)
    sibling = high * 2 + 1 - low
    me = sx * nsy + sy

    barrier = pltpu.get_barrier_semaphore()

    def greet(i, carry):
        peer = lax.rem(me + i, peers)
        pl.semaphore_signal(
            barrier, inc=1,
            device_id={"sx": lax.div(peer, nsy), "sy": lax.rem(peer, nsy)},
            device_id_type=MESH,
        )
        return carry

    for i in range(1, nvel):
        pl.semaphore_signal(
            barrier, inc=1, device_id={"vel": lax.rem(vel + i, nvel)}, device_id_type=MESH
        )
    lax.fori_loop(1, peers, greet, 0)

    def piece(k):
        return f_hbm.at[
            k // per_row, pl.ds(pl.multiple_of((k % per_row) * GROUP, GROUP), GROUP), :
        ]

    def cells_of(r, core):
        return f_hbm.at[r, pl.ds(pl.multiple_of(core * GROUP, GROUP), GROUP), :]

    half_lanes = pl.ds(pl.multiple_of(low * HALF, HALF), HALF)
    sib_lanes = pl.ds(pl.multiple_of((1 - low) * HALF, HALF), HALF)

    def share_rows(owner):
        return pl.ds(pl.multiple_of(owner * share, share), share)

    def load_own(k):
        return pltpu.make_async_copy(piece(k), own.at[k], loc_sem.at[k])

    def load_part(r):
        return pltpu.make_async_copy(
            cells_of(r, low), tiles.at[low, r], part_sem.at[r]
        )

    own_weights = pltpu.make_async_copy(
        w_hbm.at[:, half_lanes], weights.at[share_rows(me), half_lanes], wloc_sem
    )
    for k in range(chunks):
        load_own(k).start()
    for r in range(tile_rows):
        load_part(r).start()
    own_weights.start()
    pl.semaphore_wait(barrier, peers + nvel - 2)

    def give(r, i, core):
        return pltpu.make_async_remote_copy(
            src_ref=cells_of(r, core),
            dst_ref=tiles.at[lax.rem(nh - i, nh) * 2 + low, r],
            send_sem=x_send.at[i * 2 + core, r],
            recv_sem=x_recv.at[lax.rem(nh - i, nh) * 2 + low, r],
            device_id={"vel": lax.rem(high + i, nh) * 2 + core}, device_id_type=MESH,
        )

    def take(r, i, core):
        return pltpu.make_async_remote_copy(
            src_ref=cells_of(r, core), dst_ref=tiles.at[i * 2 + core, r],
            send_sem=x_send.at[i * 2 + core, r], recv_sem=x_recv.at[i * 2 + core, r],
            device_id={"vel": lax.rem(high + i, nh) * 2 + core}, device_id_type=MESH,
        )

    def give_back(r):
        return pltpu.make_async_remote_copy(
            src_ref=back_out.at[r], dst_ref=back_in.at[r],
            send_sem=back_send.at[r], recv_sem=back_recv.at[r],
            device_id={"vel": sibling}, device_id_type=MESH,
        )

    def send_weights(i):
        peer = lax.rem(me + i, peers)
        return pltpu.make_async_remote_copy(
            src_ref=w_hbm.at[:, half_lanes], dst_ref=weights.at[share_rows(me), half_lanes],
            send_sem=w_send.at[peer], recv_sem=w_recv.at[me],
            device_id={"sx": lax.div(peer, nsy), "sy": lax.rem(peer, nsy)},
            device_id_type=MESH,
        )

    def take_weights(i):
        peer = lax.rem(me + i, peers)
        return pltpu.make_async_remote_copy(
            src_ref=w_hbm.at[:, half_lanes], dst_ref=weights.at[share_rows(peer), half_lanes],
            send_sem=w_send.at[peer], recv_sem=w_recv.at[peer],
            device_id={"sx": lax.div(peer, nsy), "sy": lax.rem(peer, nsy)},
            device_id_type=MESH,
        )

    def swap_weights(lanes):
        return pltpu.make_async_remote_copy(
            src_ref=weights.at[:, lanes], dst_ref=weights.at[:, lanes],
            send_sem=wf_sem.at[0], recv_sem=wf_sem.at[1],
            device_id={"vel": sibling}, device_id_type=MESH,
        )

    def row_halo(way):
        target = lax.rem(sx + (1 if way == 0 else nsx - 1), nsx)
        return pltpu.make_async_remote_copy(
            src_ref=row_out.at[way], dst_ref=row_in.at[way],
            send_sem=halo_send.at[way], recv_sem=halo_recv.at[way],
            device_id={"sx": target}, device_id_type=MESH,
        )

    def col_halo(way):
        target = lax.rem(sy + (1 if way == 0 else nsy - 1), nsy)
        return pltpu.make_async_remote_copy(
            src_ref=col_out.at[way], dst_ref=col_in.at[way],
            send_sem=halo_send.at[2 + way], recv_sem=halo_recv.at[2 + way],
            device_id={"sy": target}, device_id_type=MESH,
        )

    for r in range(tile_rows):
        for i in range(1, nh):
            for core in range(2):
                give(r, i, core).start()
        give(r, 0, 1 - low).start()

    def start_weights(i, carry):
        send_weights(i).start()
        return carry

    lax.fori_loop(1, peers, start_weights, 0)

    for k in range(chunks):
        load_own(k).wait()

    for z in range(depth):
        for j in range(per_row):
            rows = slice(j * GROUP, (j + 1) * GROUP)
            lanes = slice(z * HALF, (z + 1) * HALF)
            row_out[0, rows, lanes] = own[
                (tile_rows - 1) * per_row + j, :, z * NXY + HALF:(z + 1) * NXY
            ]
            row_out[1, rows, lanes] = own[j, :, z * NXY:z * NXY + HALF]
    row_halo(0).start()
    row_halo(1).start()
    packed = col_out.shape[1]
    edge = depth * tile_rows * GROUP
    for way, (part, line) in enumerate(((per_row - 1, GROUP - 1), (0, 0))):
        stack = jnp.concatenate(
            [
                own[r * per_row + part, :, z * NXY:(z + 1) * NXY]
                for r in range(tile_rows)
                for z in range(depth)
            ],
            axis=0,
        )
        pick = (
            lax.broadcasted_iota(jnp.int32, (packed, edge), 1)
            == lax.broadcasted_iota(jnp.int32, (packed, edge), 0) * GROUP + line
        )
        pick = jnp.where(pick, 1.0, 0.0).astype(BF16)
        col_out[way] = jnp.dot(pick, stack, preferred_element_type=F32).astype(BF16)
        col_halo(way).start()

    rows, cols = spread.shape
    chip_first = high * 2 * depth
    plane_row = lax.broadcasted_iota(jnp.int32, (rows, NVZ), 0) >> 4
    plane_row = jnp.where(
        plane_row < depth,
        plane_row + sibling * depth,
        plane_row - depth + vel * depth,
    )
    chosen = lax.broadcasted_iota(jnp.int32, (rows, NVZ), 1) == plane_row
    plane_col = (
        (lax.broadcasted_iota(jnp.int32, (NVZ, cols), 1) >> 4) + chip_first
    ) & (NVZ - 1)
    fan = lax.broadcasted_iota(jnp.int32, (NVZ, cols), 0) == plane_col
    picked = jnp.dot(
        jnp.where(chosen, 1.0, 0.0).astype(BF16), d_ref[...], preferred_element_type=F32
    ).astype(BF16)
    wide = jnp.dot(picked, jnp.where(fan, 1.0, 0.0).astype(BF16), preferred_element_type=F32)
    same = (
        lax.broadcasted_iota(jnp.int32, (rows, cols), 0) & (GROUP - 1)
    ) == (lax.broadcasted_iota(jnp.int32, (rows, cols), 1) & (GROUP - 1))
    spread[...] = jnp.where(same, wide, 0.0).astype(BF16)

    across, along = lane_speeds((NXY, 128), 0)
    column = lax.broadcasted_iota(jnp.int32, (NXY, 128), 1)
    square = across * across + along * along
    coarse = square.astype(BF16).astype(F32)
    probe = jnp.where(column == 0, 1.0, 0.0)
    probe = jnp.where(column == 1, across, probe)
    probe = jnp.where(column == 2, along, probe)
    probe = jnp.where(column == 3, coarse, probe)
    probe = jnp.where(column == 4, square - coarse, probe)
    probes[...] = probe.astype(BF16)

    near = 2 * depth

    def depth_speed(q):
        plane = lax.rem(chip_first + q, NVZ)
        return (plane.astype(F32) - (NVZ - 1) / 2.0) * (8.0 / NVZ)

    vz = [depth_speed(q) for q in range(NVZ)]

    def stack_of(r, first, last):
        return jnp.concatenate(
            [
                tiles[v, r, :, z * NXY:(z + 1) * NXY]
                for v in range(first, last)
                for z in range(depth)
            ],
            axis=0,
        )

    def moments(stack, first, last, start):
        sums = jnp.dot(stack, probes[...], preferred_element_type=F32)
        plain, first_order, second_order = start
        for q in range(first, last):
            term = sums[(q - first) * GROUP:(q - first + 1) * GROUP]
            plain = plain + term
            first_order = first_order + vz[q] * term
            second_order = second_order + (vz[q] * vz[q]) * term
        return plain, first_order, second_order

    def prepare(r, carry):
        load_part(r).wait()
        take(r, 0, 1 - low).wait_recv()
        stack = stack_of(r, 0, 2)
        zero = jnp.zeros((GROUP, 128), F32)
        for index, block in enumerate(moments(stack, 0, near, (zero, zero, zero))):
            near_sums[r, index] = block
        near_mix[r] = jnp.dot(
            spread[:, :near * GROUP], stack, preferred_element_type=F32
        )
        return carry

    def relax(r):
        for i in range(1, nh):
            for core in range(2):
                take(r, i, core).wait_recv()
        stack = stack_of(r, 2, nvel)
        plain, first_order, second_order = moments(
            stack, near, NVZ, tuple(near_sums[r, index] for index in range(3))
        )

        def lanes(block, q):
            return jnp.broadcast_to(block[:, q:q + 1], (GROUP, 128))

        density = lanes(plain, 0)
        ux = lanes(plain, 1) / density
        uy = lanes(plain, 2) / density
        uz = lanes(first_order, 0) / density
        energy = lanes(plain, 3) + lanes(plain, 4) + lanes(second_order, 0)
        heat = (energy / density - (ux * ux + uy * uy + uz * uz)) / 3.0
        spread_heat = (2.0 * math.pi) * heat
        volume = (8.0 / NVX) * (8.0 / NVY) * (8.0 / NVZ)
        scale = density * volume / (spread_heat * jnp.sqrt(spread_heat))
        rate = 0.5 / heat

        def wider(block, count):
            return jnp.concatenate([block] * count, axis=1)

        vx, vy = lane_speeds((GROUP, NXY), 1)
        gap_x = vx - wider(ux, NXY // 128)
        gap_y = vy - wider(uy, NXY // 128)
        plane = jnp.exp(-(gap_x * gap_x + gap_y * gap_y) * wider(rate, NXY // 128))
        column = jnp.concatenate(
            [scale * jnp.exp(-((vz[w] - uz) * (vz[w] - uz)) * rate) for w in range(NVZ)], axis=0
        )
        head = column.astype(BF16)
        rest = (column - head.astype(F32)).astype(BF16)
        depth_mix = jnp.dot(spread[...], head, preferred_element_type=F32) + jnp.dot(
            spread[...], rest, preferred_element_type=F32
        )
        mix = near_mix[r] + jnp.dot(
            spread[:, near * GROUP:], stack, preferred_element_type=F32
        )
        even = wider(depth_mix, NXY // 128) * jnp.concatenate([plane] * near, axis=0)
        mixed[r] = (even - mix).astype(BF16)

    vx, vy = lane_speeds((1, NXY), 1)
    pace_x, pace_y = jnp.abs(vx), jnp.abs(vy)
    toward = vy > 0.0

    def transport():
        for way in range(2):
            row_halo(way).wait_recv()
            col_halo(way).wait_recv()
        col_wide[...] = col_in[...].astype(F32)
        line = lax.broadcasted_iota(jnp.int32, (tile_cols, NXY), 0)
        for r in range(tile_rows):

            def plane_step(z, carry):
                whole = pl.ds(pl.multiple_of(z * NXY, NXY), NXY)
                left_half = pl.ds(pl.multiple_of(z * NXY, HALF), HALF)
                right_half = pl.ds(pl.multiple_of(z * NXY + HALF, HALF), HALF)
                packed_half = pl.ds(pl.multiple_of(z * HALF, HALF), HALF)

                def row(index, lanes):
                    return jnp.concatenate(
                        [own[index * per_row + j, :, lanes] for j in range(per_row)],
                        axis=0,
                    ).astype(F32)

                current = row(r, whole)
                place = pl.ds(r * depth + z, 1)
                left = jnp.where(line == 0, col_wide[0, place, :], pltpu.roll(current, 1, 0))
                right = jnp.where(
                    line == tile_cols - 1,
                    col_wide[1, place, :],
                    pltpu.roll(current, tile_cols - 1, 0),
                )
                if r == tile_rows - 1:
                    upper = row_in[1, :, packed_half].astype(F32)
                else:
                    upper = row(r + 1, left_half)
                if r == 0:
                    lower = row_in[0, :, packed_half].astype(F32)
                else:
                    lower = row(r - 1, right_half)
                across = pace_x * (current - jnp.concatenate([upper, lower], axis=1))
                along = pace_y * (current - jnp.where(toward, left, right))
                moved = current - (
                    COURANT / (4.0 - 4.0 / NVX) * across + COURANT / (4.0 - 4.0 / NVY) * along
                )
                for j in range(per_row):
                    base[r * per_row + j, :, whole] = moved[j * GROUP:(j + 1) * GROUP]
                return carry

            lax.fori_loop(0, depth, plane_step, 0)

    def store(k):
        return pltpu.make_async_copy(
            result.at[k],
            out_hbm.at[
                k // per_row, pl.ds(pl.multiple_of((k % per_row) * GROUP, GROUP), GROUP), :
            ],
            out_sem.at[k],
        )

    def through_plane(block):
        return lax.dot_general(
            block, weights[...], (((1,), (1,)), ((), ())), preferred_element_type=F32
        )

    def finish(r, core, collision):
        k = r * per_row + core
        for z in range(depth):
            lanes = slice(z * NXY, (z + 1) * NXY)
            result[k, :, lanes] = (
                base[k, :, lanes] + RELAX_RATE * collision[z * GROUP:(z + 1) * GROUP]
            ).astype(BF16)
        store(k).start()

    half_rows = depth * GROUP

    def collide(r):
        back_out[r] = through_plane(mixed[r, :half_rows]).astype(BF16)
        give_back(r).start()
        finish(r, low, through_plane(mixed[r, half_rows:]))
        give_back(r).wait_recv()
        finish(r, 1 - low, back_in[r].astype(F32))

    lax.fori_loop(0, tile_rows, prepare, 0)
    own_weights.wait()

    def await_weights(i, carry):
        take_weights(i).wait_recv()
        return carry

    def step(r, carry):
        relax(r)

        @pl.when(r == 0)
        def _():
            lax.fori_loop(1, peers, await_weights, 0)
            swap_weights(half_lanes).start()
            transport()
            swap_weights(sib_lanes).wait_recv()

        collide(r)
        return carry

    lax.fori_loop(0, tile_rows, step, 0)

    for r in range(tile_rows):
        for i in range(1, nh):
            for core in range(2):
                give(r, i, core).wait_send()
        give(r, 0, 1 - low).wait_send()
        give_back(r).wait_send()
    for k in range(chunks):
        store(k).wait()

    def sent(i, carry):
        send_weights(i).wait_send()
        return carry

    lax.fori_loop(1, peers, sent, 0)
    swap_weights(half_lanes).wait_send()
    for way in range(2):
        row_halo(way).wait_send()
        col_halo(way).wait_send()


def local(sizes, distribution, plane_weights, depth_weights):
    nvel, nsx, nsy = sizes
    tile_rows, tile_cols, width = distribution.shape
    depth = width // NXY
    chunks = tile_rows * tile_cols // GROUP
    packed = -(-tile_rows * depth // 16) * 16
    dma = pltpu.SemaphoreType.DMA
    cells = tile_rows * tile_cols
    return pl.pallas_call(
        functools.partial(kernel, sizes),
        out_shape=jax.ShapeDtypeStruct(distribution.shape, BF16),
        in_specs=[
            pl.BlockSpec(memory_space=pl.ANY),
            pl.BlockSpec(memory_space=pl.ANY),
            pl.BlockSpec(memory_space=pltpu.VMEM),
        ],
        out_specs=pl.BlockSpec(memory_space=pl.ANY),
        scratch_shapes=[
            pltpu.VMEM((chunks, GROUP, width), BF16),
            pltpu.VMEM((nvel, tile_rows, GROUP, width), BF16),
            pltpu.VMEM((NXY, NXY), BF16),
            pltpu.VMEM((chunks, GROUP, width), F32),
            pltpu.VMEM((tile_rows, 2 * GROUP * depth, NXY), BF16),
            pltpu.VMEM((chunks, GROUP, width), BF16),
            pltpu.VMEM((2 * GROUP * depth, GROUP * NVZ), BF16),
            pltpu.VMEM((NXY, 128), BF16),
            pltpu.VMEM((tile_rows, 2 * GROUP * depth, NXY), F32),
            pltpu.VMEM((tile_rows, 3, GROUP, 128), F32),
            pltpu.VMEM((tile_rows, GROUP * depth, NXY), BF16),
            pltpu.VMEM((tile_rows, GROUP * depth, NXY), BF16),
            pltpu.VMEM((2, tile_cols, depth * HALF), BF16),
            pltpu.VMEM((2, tile_cols, depth * HALF), BF16),
            pltpu.VMEM((2, packed, NXY), BF16),
            pltpu.VMEM((2, packed, NXY), BF16),
            pltpu.VMEM((2, packed, NXY), F32),
            dma((chunks,)),
            dma((tile_rows,)),
            dma,
            dma((nvel, tile_rows)),
            dma((nvel, tile_rows)),
            dma((tile_rows,)),
            dma((tile_rows,)),
            dma((nsx * nsy,)),
            dma((nsx * nsy,)),
            dma((2,)),
            dma((4,)),
            dma((4,)),
            dma((chunks,)),
        ],
        compiler_params=pltpu.CompilerParams(
            collective_id=0, has_side_effects=True, vmem_limit_bytes=56 * 1024 * 1024
        ),
        cost_estimate=pl.CostEstimate(
            flops=2 * cells * depth * NXY * NXY,
            bytes_accessed=4 * cells * width,
            transcendentals=cells * NXY,
        ),
    )(distribution, plane_weights, depth_weights)


def solution(mesh):
    sizes = (mesh.shape["vel"], mesh.shape["sx"], mesh.shape["sy"])
    return jax.shard_map(
        functools.partial(local, sizes),
        mesh=mesh,
        in_specs=(P("sx", "sy", "vel"), P(("sx", "sy"), None), P()),
        out_specs=P("sx", "sy", "vel"),
        check_vma=False,
    )
```

```python
import functools
import math

import jax
import jax.numpy as jnp
from jax import lax
from jax.experimental import pallas as pl
from jax.experimental.pallas import tpu as pltpu
from jax.sharding import PartitionSpec as P

NVZ = 32
NVX = 32
NVY = 32
NXY = NVX * NVY
HALF = NXY // 2
GROUP = 16
COURANT = 0.45
RELAX_RATE = 0.3
MESH = pl.DeviceIdType.MESH
F32 = jnp.float32
BF16 = jnp.bfloat16


def lane_speeds(shape, dim):
    lane = lax.broadcasted_iota(jnp.int32, shape, dim)
    across = ((lane >> 5).astype(F32) - (NVX - 1) / 2.0) * (8.0 / NVX)
    along = ((lane & 31).astype(F32) - (NVY - 1) / 2.0) * (8.0 / NVY)
    return across, along


def kernel(
    sizes, f_hbm, w_hbm, d_ref, out_hbm,
    own, tiles, weights, turned, base, mixed, result, spread, probes, near_mix, near_sums,
    back_out, back_in,
    row_out, row_in, col_out, col_in, col_wide,
    loc_sem, part_sem, wloc_sem, x_send, x_recv, back_send, back_recv,
    w_send, w_recv, wf_sem, halo_send, halo_recv, out_sem,
):
    nvel, nsx, nsy = sizes
    nh = nvel // 2
    peers = nsx * nsy
    tile_rows, tile_cols, _ = f_hbm.shape
    depth = NVZ // nvel
    per_row = tile_cols // GROUP
    chunks = tile_rows * per_row
    share = NXY // peers
    vel = lax.axis_index("vel")
    sx = lax.axis_index("sx")
    sy = lax.axis_index("sy")
    high, low = lax.div(vel, 2), lax.rem(vel, 2)
    sibling = high * 2 + 1 - low
    me = sx * nsy + sy

    barrier = pltpu.get_barrier_semaphore()

    def greet(i, carry):
        peer = lax.rem(me + i, peers)
        pl.semaphore_signal(
            barrier, inc=1,
            device_id={"sx": lax.div(peer, nsy), "sy": lax.rem(peer, nsy)},
            device_id_type=MESH,
        )
        return carry

    for i in range(1, nvel):
        pl.semaphore_signal(
            barrier, inc=1, device_id={"vel": lax.rem(vel + i, nvel)}, device_id_type=MESH
        )
    lax.fori_loop(1, peers, greet, 0)

    def piece(k):
        return f_hbm.at[
            k // per_row, pl.ds(pl.multiple_of((k % per_row) * GROUP, GROUP), GROUP), :
        ]

    def cells_of(r, core):
        return f_hbm.at[r, pl.ds(pl.multiple_of(core * GROUP, GROUP), GROUP), :]

    half_lanes = pl.ds(pl.multiple_of(low * HALF, HALF), HALF)
    sib_lanes = pl.ds(pl.multiple_of((1 - low) * HALF, HALF), HALF)

    def share_rows(owner):
        return pl.ds(pl.multiple_of(owner * share, share), share)

    def load_own(k):
        return pltpu.make_async_copy(piece(k), own.at[k], loc_sem.at[k])

    def load_part(r):
        return pltpu.make_async_copy(
            cells_of(r, low), tiles.at[low, r], part_sem.at[r]
        )

    own_weights = pltpu.make_async_copy(
        w_hbm.at[:, half_lanes], weights.at[share_rows(me), half_lanes], wloc_sem
    )
    for k in range(chunks):
        load_own(k).start()
    for r in range(tile_rows):
        load_part(r).start()
    own_weights.start()
    pl.semaphore_wait(barrier, peers + nvel - 2)

    def give(r, i, core):
        return pltpu.make_async_remote_copy(
            src_ref=cells_of(r, core),
            dst_ref=tiles.at[lax.rem(nh - i, nh) * 2 + low, r],
            send_sem=x_send.at[i * 2 + core, r],
            recv_sem=x_recv.at[lax.rem(nh - i, nh) * 2 + low, r],
            device_id={"vel": lax.rem(high + i, nh) * 2 + core}, device_id_type=MESH,
        )

    def take(r, i, core):
        return pltpu.make_async_remote_copy(
            src_ref=cells_of(r, core), dst_ref=tiles.at[i * 2 + core, r],
            send_sem=x_send.at[i * 2 + core, r], recv_sem=x_recv.at[i * 2 + core, r],
            device_id={"vel": lax.rem(high + i, nh) * 2 + core}, device_id_type=MESH,
        )

    def give_back(r):
        return pltpu.make_async_remote_copy(
            src_ref=back_out.at[r], dst_ref=back_in.at[r],
            send_sem=back_send.at[r], recv_sem=back_recv.at[r],
            device_id={"vel": sibling}, device_id_type=MESH,
        )

    def send_weights(i):
        peer = lax.rem(me + i, peers)
        return pltpu.make_async_remote_copy(
            src_ref=w_hbm.at[:, half_lanes], dst_ref=weights.at[share_rows(me), half_lanes],
            send_sem=w_send.at[peer], recv_sem=w_recv.at[me],
            device_id={"sx": lax.div(peer, nsy), "sy": lax.rem(peer, nsy)},
            device_id_type=MESH,
        )

    def take_weights(i):
        peer = lax.rem(me + i, peers)
        return pltpu.make_async_remote_copy(
            src_ref=w_hbm.at[:, half_lanes], dst_ref=weights.at[share_rows(peer), half_lanes],
            send_sem=w_send.at[peer], recv_sem=w_recv.at[peer],
            device_id={"sx": lax.div(peer, nsy), "sy": lax.rem(peer, nsy)},
            device_id_type=MESH,
        )

    def swap_weights(lanes):
        return pltpu.make_async_remote_copy(
            src_ref=weights.at[:, lanes], dst_ref=weights.at[:, lanes],
            send_sem=wf_sem.at[0], recv_sem=wf_sem.at[1],
            device_id={"vel": sibling}, device_id_type=MESH,
        )

    def row_halo(way):
        target = lax.rem(sx + (1 if way == 0 else nsx - 1), nsx)
        return pltpu.make_async_remote_copy(
            src_ref=row_out.at[way], dst_ref=row_in.at[way],
            send_sem=halo_send.at[way], recv_sem=halo_recv.at[way],
            device_id={"sx": target}, device_id_type=MESH,
        )

    def col_halo(way):
        target = lax.rem(sy + (1 if way == 0 else nsy - 1), nsy)
        return pltpu.make_async_remote_copy(
            src_ref=col_out.at[way], dst_ref=col_in.at[way],
            send_sem=halo_send.at[2 + way], recv_sem=halo_recv.at[2 + way],
            device_id={"sy": target}, device_id_type=MESH,
        )

    for r in range(tile_rows):
        for i in range(1, nh):
            for core in range(2):
                give(r, i, core).start()
        give(r, 0, 1 - low).start()

    def start_weights(i, carry):
        send_weights(i).start()
        return carry

    lax.fori_loop(1, peers, start_weights, 0)

    for k in range(chunks):
        load_own(k).wait()

    for z in range(depth):
        for j in range(per_row):
            rows = slice(j * GROUP, (j + 1) * GROUP)
            lanes = slice(z * HALF, (z + 1) * HALF)
            row_out[0, rows, lanes] = own[
                (tile_rows - 1) * per_row + j, :, z * NXY + HALF:(z + 1) * NXY
            ]
            row_out[1, rows, lanes] = own[j, :, z * NXY:z * NXY + HALF]
    row_halo(0).start()
    row_halo(1).start()
    packed = col_out.shape[1]
    edge = depth * tile_rows * GROUP
    for way, (part, line) in enumerate(((per_row - 1, GROUP - 1), (0, 0))):
        stack = jnp.concatenate(
            [
                own[r * per_row + part, :, z * NXY:(z + 1) * NXY]
                for r in range(tile_rows)
                for z in range(depth)
            ],
            axis=0,
        )
        pick = (
            lax.broadcasted_iota(jnp.int32, (packed, edge), 1)
            == lax.broadcasted_iota(jnp.int32, (packed, edge), 0) * GROUP + line
        )
        pick = jnp.where(pick, 1.0, 0.0).astype(BF16)
        col_out[way] = jnp.dot(pick, stack, preferred_element_type=F32).astype(BF16)
        col_halo(way).start()

    rows, cols = spread.shape
    chip_first = high * 2 * depth
    plane_row = lax.broadcasted_iota(jnp.int32, (rows, NVZ), 0) >> 4
    plane_row = jnp.where(
        plane_row < depth,
        plane_row + sibling * depth,
        plane_row - depth + vel * depth,
    )
    chosen = lax.broadcasted_iota(jnp.int32, (rows, NVZ), 1) == plane_row
    plane_col = (
        (lax.broadcasted_iota(jnp.int32, (NVZ, cols), 1) >> 4) + chip_first
    ) & (NVZ - 1)
    fan = lax.broadcasted_iota(jnp.int32, (NVZ, cols), 0) == plane_col
    picked = jnp.dot(
        jnp.where(chosen, 1.0, 0.0).astype(BF16), d_ref[...], preferred_element_type=F32
    ).astype(BF16)
    wide = jnp.dot(picked, jnp.where(fan, 1.0, 0.0).astype(BF16), preferred_element_type=F32)
    same = (
        lax.broadcasted_iota(jnp.int32, (rows, cols), 0) & (GROUP - 1)
    ) == (lax.broadcasted_iota(jnp.int32, (rows, cols), 1) & (GROUP - 1))
    spread[...] = jnp.where(same, wide, 0.0).astype(BF16)

    across, along = lane_speeds((NXY, 128), 0)
    column = lax.broadcasted_iota(jnp.int32, (NXY, 128), 1)
    square = across * across + along * along
    coarse = square.astype(BF16).astype(F32)
    probe = jnp.where(column == 0, 1.0, 0.0)
    probe = jnp.where(column == 1, across, probe)
    probe = jnp.where(column == 2, along, probe)
    probe = jnp.where(column == 3, coarse, probe)
    probe = jnp.where(column == 4, square - coarse, probe)
    probes[...] = probe.astype(BF16)

    near = 2 * depth

    def depth_speed(q):
        plane = lax.rem(chip_first + q, NVZ)
        return (plane.astype(F32) - (NVZ - 1) / 2.0) * (8.0 / NVZ)

    vz = [depth_speed(q) for q in range(NVZ)]

    def stack_of(r, first, last):
        return jnp.concatenate(
            [
                tiles[v, r, :, z * NXY:(z + 1) * NXY]
                for v in range(first, last)
                for z in range(depth)
            ],
            axis=0,
        )

    def moments(stack, first, last, start):
        sums = jnp.dot(stack, probes[...], preferred_element_type=F32)
        plain, first_order, second_order = start
        for q in range(first, last):
            term = sums[(q - first) * GROUP:(q - first + 1) * GROUP]
            plain = plain + term
            first_order = first_order + vz[q] * term
            second_order = second_order + (vz[q] * vz[q]) * term
        return plain, first_order, second_order

    def prepare(r, carry):
        load_part(r).wait()
        take(r, 0, 1 - low).wait_recv()
        stack = stack_of(r, 0, 2)
        zero = jnp.zeros((GROUP, 128), F32)
        for index, block in enumerate(moments(stack, 0, near, (zero, zero, zero))):
            near_sums[r, index] = block
        near_mix[r] = jnp.dot(
            spread[:, :near * GROUP], stack, preferred_element_type=F32
        )
        return carry

    def relax(r):
        for i in range(1, nh):
            for core in range(2):
                take(r, i, core).wait_recv()
        stack = stack_of(r, 2, nvel)
        plain, first_order, second_order = moments(
            stack, near, NVZ, tuple(near_sums[r, index] for index in range(3))
        )

        def lanes(block, q):
            return jnp.broadcast_to(block[:, q:q + 1], (GROUP, 128))

        density = lanes(plain, 0)
        ux = lanes(plain, 1) / density
        uy = lanes(plain, 2) / density
        uz = lanes(first_order, 0) / density
        energy = lanes(plain, 3) + lanes(plain, 4) + lanes(second_order, 0)
        heat = (energy / density - (ux * ux + uy * uy + uz * uz)) / 3.0
        spread_heat = (2.0 * math.pi) * heat
        volume = (8.0 / NVX) * (8.0 / NVY) * (8.0 / NVZ)
        scale = density * volume / (spread_heat * jnp.sqrt(spread_heat))
        rate = 0.5 / heat

        def wider(block, count):
            return jnp.concatenate([block] * count, axis=1)

        vx, vy = lane_speeds((GROUP, NXY), 1)
        gap_x = vx - wider(ux, NXY // 128)
        gap_y = vy - wider(uy, NXY // 128)
        plane = jnp.exp(-(gap_x * gap_x + gap_y * gap_y) * wider(rate, NXY // 128))
        column = jnp.concatenate(
            [scale * jnp.exp(-((vz[w] - uz) * (vz[w] - uz)) * rate) for w in range(NVZ)], axis=0
        )
        head = column.astype(BF16)
        rest = (column - head.astype(F32)).astype(BF16)
        depth_mix = jnp.dot(spread[...], head, preferred_element_type=F32) + jnp.dot(
            spread[...], rest, preferred_element_type=F32
        )
        mix = near_mix[r] + jnp.dot(
            spread[:, near * GROUP:], stack, preferred_element_type=F32
        )
        even = wider(depth_mix, NXY // 128) * jnp.concatenate([plane] * near, axis=0)
        mixed[r] = (even - mix).astype(BF16)

    vx, vy = lane_speeds((1, NXY), 1)
    pace_x, pace_y = jnp.abs(vx), jnp.abs(vy)
    toward = vy > 0.0

    def transport():
        for way in range(2):
            row_halo(way).wait_recv()
            col_halo(way).wait_recv()
        col_wide[...] = col_in[...].astype(F32)
        line = lax.broadcasted_iota(jnp.int32, (tile_cols, NXY), 0)
        for r in range(tile_rows):

            def plane_step(z, carry):
                whole = pl.ds(pl.multiple_of(z * NXY, NXY), NXY)
                left_half = pl.ds(pl.multiple_of(z * NXY, HALF), HALF)
                right_half = pl.ds(pl.multiple_of(z * NXY + HALF, HALF), HALF)
                packed_half = pl.ds(pl.multiple_of(z * HALF, HALF), HALF)

                def row(index, lanes):
                    return jnp.concatenate(
                        [own[index * per_row + j, :, lanes] for j in range(per_row)],
                        axis=0,
                    ).astype(F32)

                current = row(r, whole)
                place = pl.ds(r * depth + z, 1)
                left = jnp.where(line == 0, col_wide[0, place, :], pltpu.roll(current, 1, 0))
                right = jnp.where(
                    line == tile_cols - 1,
                    col_wide[1, place, :],
                    pltpu.roll(current, tile_cols - 1, 0),
                )
                if r == tile_rows - 1:
                    upper = row_in[1, :, packed_half].astype(F32)
                else:
                    upper = row(r + 1, left_half)
                if r == 0:
                    lower = row_in[0, :, packed_half].astype(F32)
                else:
                    lower = row(r - 1, right_half)
                across = pace_x * (current - jnp.concatenate([upper, lower], axis=1))
                along = pace_y * (current - jnp.where(toward, left, right))
                moved = current - (
                    COURANT / (4.0 - 4.0 / NVX) * across + COURANT / (4.0 - 4.0 / NVY) * along
                )
                for j in range(per_row):
                    base[r * per_row + j, :, whole] = moved[j * GROUP:(j + 1) * GROUP]
                return carry

            lax.fori_loop(0, depth, plane_step, 0)

    def store(k):
        return pltpu.make_async_copy(
            result.at[k],
            out_hbm.at[
                k // per_row, pl.ds(pl.multiple_of((k % per_row) * GROUP, GROUP), GROUP), :
            ],
            out_sem.at[k],
        )

    def through_plane(block):
        return jnp.dot(block, turned[...], preferred_element_type=F32)

    def finish(r, core, collision):
        k = r * per_row + core
        for z in range(depth):
            lanes = slice(z * NXY, (z + 1) * NXY)
            result[k, :, lanes] = (
                base[k, :, lanes] + RELAX_RATE * collision[z * GROUP:(z + 1) * GROUP]
            ).astype(BF16)
        store(k).start()

    half_rows = depth * GROUP

    def collide(r):
        back_out[r] = through_plane(mixed[r, :half_rows]).astype(BF16)
        give_back(r).start()
        finish(r, low, through_plane(mixed[r, half_rows:]))
        give_back(r).wait_recv()
        finish(r, 1 - low, back_in[r].astype(F32))

    lax.fori_loop(0, tile_rows, prepare, 0)
    own_weights.wait()

    def await_weights(i, carry):
        take_weights(i).wait_recv()
        return carry

    def step(r, carry):
        relax(r)

        @pl.when(r == 0)
        def _():
            lax.fori_loop(1, peers, await_weights, 0)
            swap_weights(half_lanes).start()
            transport()
            swap_weights(sib_lanes).wait_recv()
            turned[...] = weights[...].T

        collide(r)
        return carry

    lax.fori_loop(0, tile_rows, step, 0)

    for r in range(tile_rows):
        for i in range(1, nh):
            for core in range(2):
                give(r, i, core).wait_send()
        give(r, 0, 1 - low).wait_send()
        give_back(r).wait_send()
    for k in range(chunks):
        store(k).wait()

    def sent(i, carry):
        send_weights(i).wait_send()
        return carry

    lax.fori_loop(1, peers, sent, 0)
    swap_weights(half_lanes).wait_send()
    for way in range(2):
        row_halo(way).wait_send()
        col_halo(way).wait_send()


def local(sizes, distribution, plane_weights, depth_weights):
    nvel, nsx, nsy = sizes
    tile_rows, tile_cols, width = distribution.shape
    depth = width // NXY
    chunks = tile_rows * tile_cols // GROUP
    packed = -(-tile_rows * depth // 16) * 16
    dma = pltpu.SemaphoreType.DMA
    cells = tile_rows * tile_cols
    return pl.pallas_call(
        functools.partial(kernel, sizes),
        out_shape=jax.ShapeDtypeStruct(distribution.shape, BF16),
        in_specs=[
            pl.BlockSpec(memory_space=pl.ANY),
            pl.BlockSpec(memory_space=pl.ANY),
            pl.BlockSpec(memory_space=pltpu.VMEM),
        ],
        out_specs=pl.BlockSpec(memory_space=pl.ANY),
        scratch_shapes=[
            pltpu.VMEM((chunks, GROUP, width), BF16),
            pltpu.VMEM((nvel, tile_rows, GROUP, width), BF16),
            pltpu.VMEM((NXY, NXY), BF16),
            pltpu.VMEM((NXY, NXY), BF16),
            pltpu.VMEM((chunks, GROUP, width), F32),
            pltpu.VMEM((tile_rows, 2 * GROUP * depth, NXY), BF16),
            pltpu.VMEM((chunks, GROUP, width), BF16),
            pltpu.VMEM((2 * GROUP * depth, GROUP * NVZ), BF16),
            pltpu.VMEM((NXY, 128), BF16),
            pltpu.VMEM((tile_rows, 2 * GROUP * depth, NXY), F32),
            pltpu.VMEM((tile_rows, 3, GROUP, 128), F32),
            pltpu.VMEM((tile_rows, GROUP * depth, NXY), BF16),
            pltpu.VMEM((tile_rows, GROUP * depth, NXY), BF16),
            pltpu.VMEM((2, tile_cols, depth * HALF), BF16),
            pltpu.VMEM((2, tile_cols, depth * HALF), BF16),
            pltpu.VMEM((2, packed, NXY), BF16),
            pltpu.VMEM((2, packed, NXY), BF16),
            pltpu.VMEM((2, packed, NXY), F32),
            dma((chunks,)),
            dma((tile_rows,)),
            dma,
            dma((nvel, tile_rows)),
            dma((nvel, tile_rows)),
            dma((tile_rows,)),
            dma((tile_rows,)),
            dma((nsx * nsy,)),
            dma((nsx * nsy,)),
            dma((2,)),
            dma((4,)),
            dma((4,)),
            dma((chunks,)),
        ],
        compiler_params=pltpu.CompilerParams(
            collective_id=0, has_side_effects=True, vmem_limit_bytes=40 * 1024 * 1024
        ),
        cost_estimate=pl.CostEstimate(
            flops=2 * cells * depth * NXY * NXY,
            bytes_accessed=4 * cells * width,
            transcendentals=cells * NXY,
        ),
    )(distribution, plane_weights, depth_weights)


def solution(mesh):
    sizes = (mesh.shape["vel"], mesh.shape["sx"], mesh.shape["sy"])
    return jax.shard_map(
        functools.partial(local, sizes),
        mesh=mesh,
        in_specs=(P("sx", "sy", "vel"), P(("sx", "sy"), None), P()),
        out_specs=P("sx", "sy", "vel"),
        check_vma=False,
    )
```

```python
import functools
import math

import jax
import jax.numpy as jnp
from jax import lax
from jax.experimental import pallas as pl
from jax.experimental.pallas import tpu as pltpu
from jax.sharding import PartitionSpec as P

NVZ = 32
NVX = 32
NVY = 32
NXY = NVX * NVY
HALF = NXY // 2
GROUP = 16
COURANT = 0.45
RELAX_RATE = 0.3
MESH = pl.DeviceIdType.MESH
F32 = jnp.float32
BF16 = jnp.bfloat16


def lane_speeds(shape, dim):
    lane = lax.broadcasted_iota(jnp.int32, shape, dim)
    across = ((lane >> 5).astype(F32) - (NVX - 1) / 2.0) * (8.0 / NVX)
    along = ((lane & 31).astype(F32) - (NVY - 1) / 2.0) * (8.0 / NVY)
    return across, along


def kernel(
    sizes, f_hbm, w_hbm, d_ref, out_hbm,
    own, tiles, weights, turned, base, mixed, result, spread, probes, near_mix, near_sums,
    back_out, back_in,
    row_out, row_in, col_out, col_in, col_wide,
    loc_sem, part_sem, wloc_sem, x_send, x_recv, back_send, back_recv,
    w_send, w_recv, wf_sem, halo_send, halo_recv, out_sem,
):
    nvel, nsx, nsy = sizes
    nh = nvel // 2
    peers = nsx * nsy
    tile_rows, tile_cols, _ = f_hbm.shape
    depth = NVZ // nvel
    per_row = tile_cols // GROUP
    chunks = tile_rows * per_row
    share = NXY // peers
    vel = lax.axis_index("vel")
    sx = lax.axis_index("sx")
    sy = lax.axis_index("sy")
    high, low = lax.div(vel, 2), lax.rem(vel, 2)
    sibling = high * 2 + 1 - low
    me = sx * nsy + sy

    barrier = pltpu.get_barrier_semaphore()

    def greet(i, carry):
        peer = lax.rem(me + i, peers)
        pl.semaphore_signal(
            barrier, inc=1,
            device_id={"sx": lax.div(peer, nsy), "sy": lax.rem(peer, nsy)},
            device_id_type=MESH,
        )
        return carry

    for i in range(1, nvel):
        pl.semaphore_signal(
            barrier, inc=1, device_id={"vel": lax.rem(vel + i, nvel)}, device_id_type=MESH
        )
    lax.fori_loop(1, peers, greet, 0)

    def piece(k):
        return f_hbm.at[
            k // per_row, pl.ds(pl.multiple_of((k % per_row) * GROUP, GROUP), GROUP), :
        ]

    def cells_of(r, core):
        return f_hbm.at[r, pl.ds(pl.multiple_of(core * GROUP, GROUP), GROUP), :]

    half_lanes = pl.ds(pl.multiple_of(low * HALF, HALF), HALF)
    sib_lanes = pl.ds(pl.multiple_of((1 - low) * HALF, HALF), HALF)

    def share_rows(owner):
        return pl.ds(pl.multiple_of(owner * share, share), share)

    def load_own(k):
        return pltpu.make_async_copy(piece(k), own.at[k], loc_sem.at[k])

    def load_part(r):
        return pltpu.make_async_copy(
            cells_of(r, low), tiles.at[low, r], part_sem.at[r]
        )

    own_weights = pltpu.make_async_copy(
        w_hbm.at[:, half_lanes], weights.at[share_rows(me), half_lanes], wloc_sem
    )
    for k in range(chunks):
        load_own(k).start()
    for r in range(tile_rows):
        load_part(r).start()
    own_weights.start()
    pl.semaphore_wait(barrier, peers + nvel - 2)

    def give(r, i, core):
        return pltpu.make_async_remote_copy(
            src_ref=cells_of(r, core),
            dst_ref=tiles.at[lax.rem(nh - i, nh) * 2 + low, r],
            send_sem=x_send.at[i * 2 + core, r],
            recv_sem=x_recv.at[lax.rem(nh - i, nh) * 2 + low, r],
            device_id={"vel": lax.rem(high + i, nh) * 2 + core}, device_id_type=MESH,
        )

    def take(r, i, core):
        return pltpu.make_async_remote_copy(
            src_ref=cells_of(r, core), dst_ref=tiles.at[i * 2 + core, r],
            send_sem=x_send.at[i * 2 + core, r], recv_sem=x_recv.at[i * 2 + core, r],
            device_id={"vel": lax.rem(high + i, nh) * 2 + core}, device_id_type=MESH,
        )

    def give_back(r):
        return pltpu.make_async_remote_copy(
            src_ref=back_out.at[r], dst_ref=back_in.at[r],
            send_sem=back_send.at[r], recv_sem=back_recv.at[r],
            device_id={"vel": sibling}, device_id_type=MESH,
        )

    def send_weights(i):
        peer = lax.rem(me + i, peers)
        return pltpu.make_async_remote_copy(
            src_ref=w_hbm.at[:, half_lanes], dst_ref=weights.at[share_rows(me), half_lanes],
            send_sem=w_send.at[peer], recv_sem=w_recv.at[me],
            device_id={"sx": lax.div(peer, nsy), "sy": lax.rem(peer, nsy)},
            device_id_type=MESH,
        )

    def take_weights(i):
        peer = lax.rem(me + i, peers)
        return pltpu.make_async_remote_copy(
            src_ref=w_hbm.at[:, half_lanes], dst_ref=weights.at[share_rows(peer), half_lanes],
            send_sem=w_send.at[peer], recv_sem=w_recv.at[peer],
            device_id={"sx": lax.div(peer, nsy), "sy": lax.rem(peer, nsy)},
            device_id_type=MESH,
        )

    def swap_weights(lanes):
        return pltpu.make_async_remote_copy(
            src_ref=weights.at[:, lanes], dst_ref=weights.at[:, lanes],
            send_sem=wf_sem.at[0], recv_sem=wf_sem.at[1],
            device_id={"vel": sibling}, device_id_type=MESH,
        )

    def row_halo(way):
        target = lax.rem(sx + (1 if way == 0 else nsx - 1), nsx)
        return pltpu.make_async_remote_copy(
            src_ref=row_out.at[way], dst_ref=row_in.at[way],
            send_sem=halo_send.at[way], recv_sem=halo_recv.at[way],
            device_id={"sx": target}, device_id_type=MESH,
        )

    def col_halo(way):
        target = lax.rem(sy + (1 if way == 0 else nsy - 1), nsy)
        return pltpu.make_async_remote_copy(
            src_ref=col_out.at[way], dst_ref=col_in.at[way],
            send_sem=halo_send.at[2 + way], recv_sem=halo_recv.at[2 + way],
            device_id={"sy": target}, device_id_type=MESH,
        )

    for r in range(tile_rows):
        for i in range(1, nh):
            for core in range(2):
                give(r, i, core).start()
        give(r, 0, 1 - low).start()

    def start_weights(i, carry):
        send_weights(i).start()
        return carry

    lax.fori_loop(1, peers, start_weights, 0)

    for k in range(chunks):
        load_own(k).wait()

    for z in range(depth):
        for j in range(per_row):
            rows = slice(j * GROUP, (j + 1) * GROUP)
            lanes = slice(z * HALF, (z + 1) * HALF)
            row_out[0, rows, lanes] = own[
                (tile_rows - 1) * per_row + j, :, z * NXY + HALF:(z + 1) * NXY
            ]
            row_out[1, rows, lanes] = own[j, :, z * NXY:z * NXY + HALF]
    row_halo(0).start()
    row_halo(1).start()
    packed = col_out.shape[1]
    edge = depth * tile_rows * GROUP
    for way, (part, line) in enumerate(((per_row - 1, GROUP - 1), (0, 0))):
        stack = jnp.concatenate(
            [
                own[r * per_row + part, :, z * NXY:(z + 1) * NXY]
                for r in range(tile_rows)
                for z in range(depth)
            ],
            axis=0,
        )
        pick = (
            lax.broadcasted_iota(jnp.int32, (packed, edge), 1)
            == lax.broadcasted_iota(jnp.int32, (packed, edge), 0) * GROUP + line
        )
        pick = jnp.where(pick, 1.0, 0.0).astype(BF16)
        col_out[way] = jnp.dot(pick, stack, preferred_element_type=F32).astype(BF16)
        col_halo(way).start()

    rows, cols = spread.shape
    chip_first = high * 2 * depth
    plane_row = lax.broadcasted_iota(jnp.int32, (rows, NVZ), 0) >> 4
    plane_row = jnp.where(
        plane_row < depth,
        plane_row + sibling * depth,
        plane_row - depth + vel * depth,
    )
    chosen = lax.broadcasted_iota(jnp.int32, (rows, NVZ), 1) == plane_row
    plane_col = (
        (lax.broadcasted_iota(jnp.int32, (NVZ, cols), 1) >> 4) + chip_first
    ) & (NVZ - 1)
    fan = lax.broadcasted_iota(jnp.int32, (NVZ, cols), 0) == plane_col
    picked = jnp.dot(
        jnp.where(chosen, 1.0, 0.0).astype(BF16), d_ref[...], preferred_element_type=F32
    ).astype(BF16)
    wide = jnp.dot(picked, jnp.where(fan, 1.0, 0.0).astype(BF16), preferred_element_type=F32)
    same = (
        lax.broadcasted_iota(jnp.int32, (rows, cols), 0) & (GROUP - 1)
    ) == (lax.broadcasted_iota(jnp.int32, (rows, cols), 1) & (GROUP - 1))
    spread[...] = jnp.where(same, wide, 0.0).astype(BF16)

    across, along = lane_speeds((NXY, 128), 0)
    column = lax.broadcasted_iota(jnp.int32, (NXY, 128), 1)
    square = across * across + along * along
    coarse = square.astype(BF16).astype(F32)
    probe = jnp.where(column == 0, 1.0, 0.0)
    probe = jnp.where(column == 1, across, probe)
    probe = jnp.where(column == 2, along, probe)
    probe = jnp.where(column == 3, coarse, probe)
    probe = jnp.where(column == 4, square - coarse, probe)
    probes[...] = probe.astype(BF16)

    near = 2 * depth

    def depth_speed(q):
        plane = lax.rem(chip_first + q, NVZ)
        return (plane.astype(F32) - (NVZ - 1) / 2.0) * (8.0 / NVZ)

    vz = [depth_speed(q) for q in range(NVZ)]

    def stack_of(r, first, last):
        return jnp.concatenate(
            [
                tiles[v, r, :, z * NXY:(z + 1) * NXY]
                for v in range(first, last)
                for z in range(depth)
            ],
            axis=0,
        )

    def moments(stack, first, last, start):
        sums = jnp.dot(stack, probes[...], preferred_element_type=F32)
        plain, first_order, second_order = start
        for q in range(first, last):
            term = sums[(q - first) * GROUP:(q - first + 1) * GROUP]
            plain = plain + term
            first_order = first_order + vz[q] * term
            second_order = second_order + (vz[q] * vz[q]) * term
        return plain, first_order, second_order

    def prepare(r, carry):
        load_part(r).wait()
        take(r, 0, 1 - low).wait_recv()
        stack = stack_of(r, 0, 2)
        zero = jnp.zeros((GROUP, 128), F32)
        for index, block in enumerate(moments(stack, 0, near, (zero, zero, zero))):
            near_sums[r, index] = block
        near_mix[r] = jnp.dot(
            spread[:, :near * GROUP], stack, preferred_element_type=F32
        )
        return carry

    def relax(r):
        for i in range(1, nh):
            for core in range(2):
                take(r, i, core).wait_recv()
        stack = stack_of(r, 2, nvel)
        plain, first_order, second_order = moments(
            stack, near, NVZ, tuple(near_sums[r, index] for index in range(3))
        )

        def lanes(block, q):
            return jnp.broadcast_to(block[:, q:q + 1], (GROUP, 128))

        density = lanes(plain, 0)
        ux = lanes(plain, 1) / density
        uy = lanes(plain, 2) / density
        uz = lanes(first_order, 0) / density
        energy = lanes(plain, 3) + lanes(plain, 4) + lanes(second_order, 0)
        heat = (energy / density - (ux * ux + uy * uy + uz * uz)) / 3.0
        spread_heat = (2.0 * math.pi) * heat
        volume = (8.0 / NVX) * (8.0 / NVY) * (8.0 / NVZ)
        scale = density * volume / (spread_heat * jnp.sqrt(spread_heat))
        rate = 0.5 / heat

        def wider(block, count):
            return jnp.concatenate([block] * count, axis=1)

        vx, vy = lane_speeds((GROUP, NXY), 1)
        gap_x = vx - wider(ux, NXY // 128)
        gap_y = vy - wider(uy, NXY // 128)
        plane = jnp.exp(-(gap_x * gap_x + gap_y * gap_y) * wider(rate, NXY // 128))
        column = jnp.concatenate(
            [scale * jnp.exp(-((vz[w] - uz) * (vz[w] - uz)) * rate) for w in range(NVZ)], axis=0
        )
        head = column.astype(BF16)
        rest = (column - head.astype(F32)).astype(BF16)
        depth_mix = jnp.dot(spread[...], head, preferred_element_type=F32) + jnp.dot(
            spread[...], rest, preferred_element_type=F32
        )
        mix = near_mix[r] + jnp.dot(
            spread[:, near * GROUP:], stack, preferred_element_type=F32
        )
        even = wider(depth_mix, NXY // 128) * jnp.concatenate([plane] * near, axis=0)
        mixed[r] = (even - mix).astype(BF16)

    vx, vy = lane_speeds((1, NXY), 1)
    pace_x, pace_y = jnp.abs(vx), jnp.abs(vy)
    toward = vy > 0.0

    def transport():
        for way in range(2):
            row_halo(way).wait_recv()
            col_halo(way).wait_recv()
        col_wide[...] = col_in[...].astype(F32)
        line = lax.broadcasted_iota(jnp.int32, (tile_cols, NXY), 0)
        for r in range(tile_rows):

            def plane_step(z, carry):
                whole = pl.ds(pl.multiple_of(z * NXY, NXY), NXY)
                left_half = pl.ds(pl.multiple_of(z * NXY, HALF), HALF)
                right_half = pl.ds(pl.multiple_of(z * NXY + HALF, HALF), HALF)
                packed_half = pl.ds(pl.multiple_of(z * HALF, HALF), HALF)

                def row(index, lanes):
                    return jnp.concatenate(
                        [own[index * per_row + j, :, lanes] for j in range(per_row)],
                        axis=0,
                    ).astype(F32)

                current = row(r, whole)
                place = pl.ds(r * depth + z, 1)
                left = jnp.where(line == 0, col_wide[0, place, :], pltpu.roll(current, 1, 0))
                right = jnp.where(
                    line == tile_cols - 1,
                    col_wide[1, place, :],
                    pltpu.roll(current, tile_cols - 1, 0),
                )
                if r == tile_rows - 1:
                    upper = row_in[1, :, packed_half].astype(F32)
                else:
                    upper = row(r + 1, left_half)
                if r == 0:
                    lower = row_in[0, :, packed_half].astype(F32)
                else:
                    lower = row(r - 1, right_half)
                across = pace_x * (current - jnp.concatenate([upper, lower], axis=1))
                along = pace_y * (current - jnp.where(toward, left, right))
                moved = current - (
                    COURANT / (4.0 - 4.0 / NVX) * across + COURANT / (4.0 - 4.0 / NVY) * along
                )
                for j in range(per_row):
                    base[r * per_row + j, :, whole] = moved[j * GROUP:(j + 1) * GROUP]
                return carry

            lax.fori_loop(0, depth, plane_step, 0)

    def store(k):
        return pltpu.make_async_copy(
            result.at[k],
            out_hbm.at[
                k // per_row, pl.ds(pl.multiple_of((k % per_row) * GROUP, GROUP), GROUP), :
            ],
            out_sem.at[k],
        )

    def through_plane(block):
        return jnp.dot(block, turned[...], preferred_element_type=F32)

    def finish(r, core, collision):
        k = r * per_row + core
        for z in range(depth):
            lanes = slice(z * NXY, (z + 1) * NXY)
            result[k, :, lanes] = (
                base[k, :, lanes] + RELAX_RATE * collision[z * GROUP:(z + 1) * GROUP]
            ).astype(BF16)
        store(k).start()

    half_rows = depth * GROUP

    def collide(r):
        back_out[r] = through_plane(mixed[r, :half_rows]).astype(BF16)
        give_back(r).start()
        finish(r, low, through_plane(mixed[r, half_rows:]))
        give_back(r).wait_recv()
        finish(r, 1 - low, back_in[r].astype(F32))

    lax.fori_loop(0, tile_rows, prepare, 0)
    own_weights.wait()

    def await_weights(i, carry):
        take_weights(i).wait_recv()
        return carry

    def step(r, carry):
        relax(r)

        @pl.when(r == 0)
        def _():
            lax.fori_loop(1, peers, await_weights, 0)
            swap_weights(half_lanes).start()
            transport()
            swap_weights(sib_lanes).wait_recv()
            turned[...] = weights[...].T

        collide(r)
        return carry

    lax.fori_loop(0, tile_rows, step, 0)

    for r in range(tile_rows):
        for i in range(1, nh):
            for core in range(2):
                give(r, i, core).wait_send()
        give(r, 0, 1 - low).wait_send()
        give_back(r).wait_send()
    for k in range(chunks):
        store(k).wait()

    def sent(i, carry):
        send_weights(i).wait_send()
        return carry

    lax.fori_loop(1, peers, sent, 0)
    swap_weights(half_lanes).wait_send()
    for way in range(2):
        row_halo(way).wait_send()
        col_halo(way).wait_send()


def local(sizes, distribution, plane_weights, depth_weights):
    nvel, nsx, nsy = sizes
    tile_rows, tile_cols, width = distribution.shape
    depth = width // NXY
    chunks = tile_rows * tile_cols // GROUP
    packed = -(-tile_rows * depth // 16) * 16
    dma = pltpu.SemaphoreType.DMA
    cells = tile_rows * tile_cols
    return pl.pallas_call(
        functools.partial(kernel, sizes),
        out_shape=pltpu.VMEM(distribution.shape, BF16),
        in_specs=[
            pl.BlockSpec(memory_space=pl.ANY),
            pl.BlockSpec(memory_space=pl.ANY),
            pl.BlockSpec(memory_space=pltpu.VMEM),
        ],
        out_specs=pl.BlockSpec(memory_space=pl.ANY),
        scratch_shapes=[
            pltpu.VMEM((chunks, GROUP, width), BF16),
            pltpu.VMEM((nvel, tile_rows, GROUP, width), BF16),
            pltpu.VMEM((NXY, NXY), BF16),
            pltpu.VMEM((NXY, NXY), BF16),
            pltpu.VMEM((chunks, GROUP, width), F32),
            pltpu.VMEM((tile_rows, 2 * GROUP * depth, NXY), BF16),
            pltpu.VMEM((chunks, GROUP, width), BF16),
            pltpu.VMEM((2 * GROUP * depth, GROUP * NVZ), BF16),
            pltpu.VMEM((NXY, 128), BF16),
            pltpu.VMEM((tile_rows, 2 * GROUP * depth, NXY), F32),
            pltpu.VMEM((tile_rows, 3, GROUP, 128), F32),
            pltpu.VMEM((tile_rows, GROUP * depth, NXY), BF16),
            pltpu.VMEM((tile_rows, GROUP * depth, NXY), BF16),
            pltpu.VMEM((2, tile_cols, depth * HALF), BF16),
            pltpu.VMEM((2, tile_cols, depth * HALF), BF16),
            pltpu.VMEM((2, packed, NXY), BF16),
            pltpu.VMEM((2, packed, NXY), BF16),
            pltpu.VMEM((2, packed, NXY), F32),
            dma((chunks,)),
            dma((tile_rows,)),
            dma,
            dma((nvel, tile_rows)),
            dma((nvel, tile_rows)),
            dma((tile_rows,)),
            dma((tile_rows,)),
            dma((nsx * nsy,)),
            dma((nsx * nsy,)),
            dma((2,)),
            dma((4,)),
            dma((4,)),
            dma((chunks,)),
        ],
        compiler_params=pltpu.CompilerParams(
            collective_id=0, has_side_effects=True, vmem_limit_bytes=56 * 1024 * 1024
        ),
        cost_estimate=pl.CostEstimate(
            flops=2 * cells * depth * NXY * NXY,
            bytes_accessed=4 * cells * width,
            transcendentals=cells * NXY,
        ),
    )(distribution, plane_weights, depth_weights)


def solution(mesh):
    sizes = (mesh.shape["vel"], mesh.shape["sx"], mesh.shape["sy"])
    return jax.shard_map(
        functools.partial(local, sizes),
        mesh=mesh,
        in_specs=(P("sx", "sy", "vel"), P(("sx", "sy"), None), P()),
        out_specs=P("sx", "sy", "vel"),
        check_vma=False,
    )
```

```python
import functools
import math

import jax
import jax.numpy as jnp
from jax import lax
from jax.experimental import pallas as pl
from jax.experimental.pallas import tpu as pltpu
from jax.sharding import PartitionSpec as P

NVZ = 32
NVX = 32
NVY = 32
NXY = NVX * NVY
HALF = NXY // 2
GROUP = 16
COURANT = 0.45
RELAX_RATE = 0.3
MESH = pl.DeviceIdType.MESH
F32 = jnp.float32
BF16 = jnp.bfloat16


def lane_speeds(shape, dim):
    lane = lax.broadcasted_iota(jnp.int32, shape, dim)
    across = ((lane >> 5).astype(F32) - (NVX - 1) / 2.0) * (8.0 / NVX)
    along = ((lane & 31).astype(F32) - (NVY - 1) / 2.0) * (8.0 / NVY)
    return across, along


def kernel(
    sizes, f_hbm, w_hbm, d_ref, out_hbm,
    own, tiles, weights, turned, base, mixed, result, spread, probes, near_mix, near_sums,
    back_out, back_in,
    row_out, row_in, col_out, col_in, col_wide,
    loc_sem, part_sem, wloc_sem, x_send, x_recv, back_send, back_recv,
    w_send, w_recv, wf_sem, halo_send, halo_recv, out_sem, ready_sem,
):
    nvel, nsx, nsy = sizes
    nh = nvel // 2
    peers = nsx * nsy
    tile_rows, tile_cols, _ = f_hbm.shape
    depth = NVZ // nvel
    per_row = tile_cols // GROUP
    chunks = tile_rows * per_row
    share = NXY // peers
    vel = lax.axis_index("vel")
    sx = lax.axis_index("sx")
    sy = lax.axis_index("sy")
    high, low = lax.div(vel, 2), lax.rem(vel, 2)
    sibling = high * 2 + 1 - low
    me = sx * nsy + sy

    barrier = pltpu.get_barrier_semaphore()

    order = sy * nsx + sx

    def cells_at(i):
        return {"sx": lax.rem(i, nsx), "sy": lax.div(i, nsx)}

    def greet(i, carry):
        pl.semaphore_signal(barrier, inc=1, device_id=cells_at(i), device_id_type=MESH)
        return carry

    def answer(i, carry):
        pl.semaphore_signal(ready_sem, inc=1, device_id=cells_at(i), device_id_type=MESH)
        return carry

    for i in range(1, nvel):
        pl.semaphore_signal(
            barrier, inc=1, device_id={"vel": lax.rem(vel + i, nvel)}, device_id_type=MESH
        )
    lax.fori_loop(order + 1, peers, greet, 0)

    def piece(k):
        return f_hbm.at[
            k // per_row, pl.ds(pl.multiple_of((k % per_row) * GROUP, GROUP), GROUP), :
        ]

    def cells_of(r, core):
        return f_hbm.at[r, pl.ds(pl.multiple_of(core * GROUP, GROUP), GROUP), :]

    half_lanes = pl.ds(pl.multiple_of(low * HALF, HALF), HALF)
    sib_lanes = pl.ds(pl.multiple_of((1 - low) * HALF, HALF), HALF)

    def share_rows(owner):
        return pl.ds(pl.multiple_of(owner * share, share), share)

    def load_own(k):
        return pltpu.make_async_copy(piece(k), own.at[k], loc_sem.at[k])

    def load_part(r):
        return pltpu.make_async_copy(
            cells_of(r, low), tiles.at[low, r], part_sem.at[r]
        )

    own_weights = pltpu.make_async_copy(
        w_hbm.at[:, half_lanes], weights.at[share_rows(me), half_lanes], wloc_sem
    )
    for k in range(chunks):
        load_own(k).start()
    for r in range(tile_rows):
        load_part(r).start()
    own_weights.start()
    pl.semaphore_wait(barrier, nvel - 1 + order)

    def give(r, i, core):
        return pltpu.make_async_remote_copy(
            src_ref=cells_of(r, core),
            dst_ref=tiles.at[lax.rem(nh - i, nh) * 2 + low, r],
            send_sem=x_send.at[i * 2 + core, r],
            recv_sem=x_recv.at[lax.rem(nh - i, nh) * 2 + low, r],
            device_id={"vel": lax.rem(high + i, nh) * 2 + core}, device_id_type=MESH,
        )

    def take(r, i, core):
        return pltpu.make_async_remote_copy(
            src_ref=cells_of(r, core), dst_ref=tiles.at[i * 2 + core, r],
            send_sem=x_send.at[i * 2 + core, r], recv_sem=x_recv.at[i * 2 + core, r],
            device_id={"vel": lax.rem(high + i, nh) * 2 + core}, device_id_type=MESH,
        )

    def give_back(r):
        return pltpu.make_async_remote_copy(
            src_ref=back_out.at[r], dst_ref=back_in.at[r],
            send_sem=back_send.at[r], recv_sem=back_recv.at[r],
            device_id={"vel": sibling}, device_id_type=MESH,
        )

    def send_weights(i):
        peer = lax.rem(me + i, peers)
        return pltpu.make_async_remote_copy(
            src_ref=w_hbm.at[:, half_lanes], dst_ref=weights.at[share_rows(me), half_lanes],
            send_sem=w_send.at[peer], recv_sem=w_recv.at[me],
            device_id={"sx": lax.div(peer, nsy), "sy": lax.rem(peer, nsy)},
            device_id_type=MESH,
        )

    def take_weights(i):
        peer = lax.rem(me + i, peers)
        return pltpu.make_async_remote_copy(
            src_ref=w_hbm.at[:, half_lanes], dst_ref=weights.at[share_rows(peer), half_lanes],
            send_sem=w_send.at[peer], recv_sem=w_recv.at[peer],
            device_id={"sx": lax.div(peer, nsy), "sy": lax.rem(peer, nsy)},
            device_id_type=MESH,
        )

    def swap_weights(lanes):
        return pltpu.make_async_remote_copy(
            src_ref=weights.at[:, lanes], dst_ref=weights.at[:, lanes],
            send_sem=wf_sem.at[0], recv_sem=wf_sem.at[1],
            device_id={"vel": sibling}, device_id_type=MESH,
        )

    def row_halo(way):
        target = lax.rem(sx + (1 if way == 0 else nsx - 1), nsx)
        return pltpu.make_async_remote_copy(
            src_ref=row_out.at[way], dst_ref=row_in.at[way],
            send_sem=halo_send.at[way], recv_sem=halo_recv.at[way],
            device_id={"sx": target}, device_id_type=MESH,
        )

    def col_halo(way):
        target = lax.rem(sy + (1 if way == 0 else nsy - 1), nsy)
        return pltpu.make_async_remote_copy(
            src_ref=col_out.at[way], dst_ref=col_in.at[way],
            send_sem=halo_send.at[2 + way], recv_sem=halo_recv.at[2 + way],
            device_id={"sy": target}, device_id_type=MESH,
        )

    for r in range(tile_rows):
        for i in range(1, nh):
            for core in range(2):
                give(r, i, core).start()
        give(r, 0, 1 - low).start()

    def start_weights(i, carry):
        send_weights(i).start()
        return carry

    lax.fori_loop(0, order, answer, 0)

    @pl.when(order < peers - 1)
    def _():
        pl.semaphore_wait(ready_sem, peers - 1 - order)

    lax.fori_loop(1, peers, start_weights, 0)

    for k in range(chunks):
        load_own(k).wait()

    for z in range(depth):
        for j in range(per_row):
            rows = slice(j * GROUP, (j + 1) * GROUP)
            lanes = slice(z * HALF, (z + 1) * HALF)
            row_out[0, rows, lanes] = own[
                (tile_rows - 1) * per_row + j, :, z * NXY + HALF:(z + 1) * NXY
            ]
            row_out[1, rows, lanes] = own[j, :, z * NXY:z * NXY + HALF]
    row_halo(0).start()
    row_halo(1).start()
    packed = col_out.shape[1]
    edge = depth * tile_rows * GROUP
    for way, (part, line) in enumerate(((per_row - 1, GROUP - 1), (0, 0))):
        stack = jnp.concatenate(
            [
                own[r * per_row + part, :, z * NXY:(z + 1) * NXY]
                for r in range(tile_rows)
                for z in range(depth)
            ],
            axis=0,
        )
        pick = (
            lax.broadcasted_iota(jnp.int32, (packed, edge), 1)
            == lax.broadcasted_iota(jnp.int32, (packed, edge), 0) * GROUP + line
        )
        pick = jnp.where(pick, 1.0, 0.0).astype(BF16)
        col_out[way] = jnp.dot(pick, stack, preferred_element_type=F32).astype(BF16)
        col_halo(way).start()

    rows, cols = spread.shape
    chip_first = high * 2 * depth
    plane_row = lax.broadcasted_iota(jnp.int32, (rows, NVZ), 0) >> 4
    plane_row = jnp.where(
        plane_row < depth,
        plane_row + sibling * depth,
        plane_row - depth + vel * depth,
    )
    chosen = lax.broadcasted_iota(jnp.int32, (rows, NVZ), 1) == plane_row
    plane_col = (
        (lax.broadcasted_iota(jnp.int32, (NVZ, cols), 1) >> 4) + chip_first
    ) & (NVZ - 1)
    fan = lax.broadcasted_iota(jnp.int32, (NVZ, cols), 0) == plane_col
    picked = jnp.dot(
        jnp.where(chosen, 1.0, 0.0).astype(BF16), d_ref[...], preferred_element_type=F32
    ).astype(BF16)
    wide = jnp.dot(picked, jnp.where(fan, 1.0, 0.0).astype(BF16), preferred_element_type=F32)
    same = (
        lax.broadcasted_iota(jnp.int32, (rows, cols), 0) & (GROUP - 1)
    ) == (lax.broadcasted_iota(jnp.int32, (rows, cols), 1) & (GROUP - 1))
    spread[...] = jnp.where(same, wide, 0.0).astype(BF16)

    across, along = lane_speeds((NXY, 128), 0)
    column = lax.broadcasted_iota(jnp.int32, (NXY, 128), 1)
    square = across * across + along * along
    coarse = square.astype(BF16).astype(F32)
    probe = jnp.where(column == 0, 1.0, 0.0)
    probe = jnp.where(column == 1, across, probe)
    probe = jnp.where(column == 2, along, probe)
    probe = jnp.where(column == 3, coarse, probe)
    probe = jnp.where(column == 4, square - coarse, probe)
    probes[...] = probe.astype(BF16)

    near = 2 * depth

    def depth_speed(q):
        plane = lax.rem(chip_first + q, NVZ)
        return (plane.astype(F32) - (NVZ - 1) / 2.0) * (8.0 / NVZ)

    vz = [depth_speed(q) for q in range(NVZ)]

    def stack_of(r, first, last):
        return jnp.concatenate(
            [
                tiles[v, r, :, z * NXY:(z + 1) * NXY]
                for v in range(first, last)
                for z in range(depth)
            ],
            axis=0,
        )

    def moments(stack, first, last, start):
        sums = jnp.dot(stack, probes[...], preferred_element_type=F32)
        plain, first_order, second_order = start
        for q in range(first, last):
            term = sums[(q - first) * GROUP:(q - first + 1) * GROUP]
            plain = plain + term
            first_order = first_order + vz[q] * term
            second_order = second_order + (vz[q] * vz[q]) * term
        return plain, first_order, second_order

    def prepare(r, carry):
        load_part(r).wait()
        take(r, 0, 1 - low).wait_recv()
        stack = stack_of(r, 0, 2)
        zero = jnp.zeros((GROUP, 128), F32)
        for index, block in enumerate(moments(stack, 0, near, (zero, zero, zero))):
            near_sums[r, index] = block
        near_mix[r] = jnp.dot(
            spread[:, :near * GROUP], stack, preferred_element_type=F32
        )
        return carry

    def relax(r):
        for i in range(1, nh):
            for core in range(2):
                take(r, i, core).wait_recv()
        stack = stack_of(r, 2, nvel)
        plain, first_order, second_order = moments(
            stack, near, NVZ, tuple(near_sums[r, index] for index in range(3))
        )

        def lanes(block, q):
            return jnp.broadcast_to(block[:, q:q + 1], (GROUP, 128))

        density = lanes(plain, 0)
        ux = lanes(plain, 1) / density
        uy = lanes(plain, 2) / density
        uz = lanes(first_order, 0) / density
        energy = lanes(plain, 3) + lanes(plain, 4) + lanes(second_order, 0)
        heat = (energy / density - (ux * ux + uy * uy + uz * uz)) / 3.0
        spread_heat = (2.0 * math.pi) * heat
        volume = (8.0 / NVX) * (8.0 / NVY) * (8.0 / NVZ)
        scale = density * volume / (spread_heat * jnp.sqrt(spread_heat))
        rate = 0.5 / heat

        def wider(block, count):
            return jnp.concatenate([block] * count, axis=1)

        vx, vy = lane_speeds((GROUP, NXY), 1)
        gap_x = vx - wider(ux, NXY // 128)
        gap_y = vy - wider(uy, NXY // 128)
        plane = jnp.exp(-(gap_x * gap_x + gap_y * gap_y) * wider(rate, NXY // 128))
        column = jnp.concatenate(
            [scale * jnp.exp(-((vz[w] - uz) * (vz[w] - uz)) * rate) for w in range(NVZ)], axis=0
        )
        head = column.astype(BF16)
        rest = (column - head.astype(F32)).astype(BF16)
        depth_mix = jnp.dot(spread[...], head, preferred_element_type=F32) + jnp.dot(
            spread[...], rest, preferred_element_type=F32
        )
        mix = near_mix[r] + jnp.dot(
            spread[:, near * GROUP:], stack, preferred_element_type=F32
        )
        even = wider(depth_mix, NXY // 128) * jnp.concatenate([plane] * near, axis=0)
        mixed[r] = (even - mix).astype(BF16)

    vx, vy = lane_speeds((1, NXY), 1)
    pace_x, pace_y = jnp.abs(vx), jnp.abs(vy)
    toward = vy > 0.0

    def transport():
        for way in range(2):
            row_halo(way).wait_recv()
            col_halo(way).wait_recv()
        col_wide[...] = col_in[...].astype(F32)
        line = lax.broadcasted_iota(jnp.int32, (tile_cols, NXY), 0)
        for r in range(tile_rows):

            def plane_step(z, carry):
                whole = pl.ds(pl.multiple_of(z * NXY, NXY), NXY)
                left_half = pl.ds(pl.multiple_of(z * NXY, HALF), HALF)
                right_half = pl.ds(pl.multiple_of(z * NXY + HALF, HALF), HALF)
                packed_half = pl.ds(pl.multiple_of(z * HALF, HALF), HALF)

                def row(index, lanes):
                    return jnp.concatenate(
                        [own[index * per_row + j, :, lanes] for j in range(per_row)],
                        axis=0,
                    ).astype(F32)

                current = row(r, whole)
                place = pl.ds(r * depth + z, 1)
                left = jnp.where(line == 0, col_wide[0, place, :], pltpu.roll(current, 1, 0))
                right = jnp.where(
                    line == tile_cols - 1,
                    col_wide[1, place, :],
                    pltpu.roll(current, tile_cols - 1, 0),
                )
                if r == tile_rows - 1:
                    upper = row_in[1, :, packed_half].astype(F32)
                else:
                    upper = row(r + 1, left_half)
                if r == 0:
                    lower = row_in[0, :, packed_half].astype(F32)
                else:
                    lower = row(r - 1, right_half)
                across = pace_x * (current - jnp.concatenate([upper, lower], axis=1))
                along = pace_y * (current - jnp.where(toward, left, right))
                moved = current - (
                    COURANT / (4.0 - 4.0 / NVX) * across + COURANT / (4.0 - 4.0 / NVY) * along
                )
                for j in range(per_row):
                    base[r * per_row + j, :, whole] = moved[j * GROUP:(j + 1) * GROUP]
                return carry

            lax.fori_loop(0, depth, plane_step, 0)

    def store(k):
        return pltpu.make_async_copy(
            result.at[k],
            out_hbm.at[
                k // per_row, pl.ds(pl.multiple_of((k % per_row) * GROUP, GROUP), GROUP), :
            ],
            out_sem.at[k],
        )

    def through_plane(block):
        return jnp.dot(block, turned[...], preferred_element_type=F32)

    def finish(r, core, collision):
        k = r * per_row + core
        for z in range(depth):
            lanes = slice(z * NXY, (z + 1) * NXY)
            result[k, :, lanes] = (
                base[k, :, lanes] + RELAX_RATE * collision[z * GROUP:(z + 1) * GROUP]
            ).astype(BF16)
        store(k).start()

    half_rows = depth * GROUP

    def collide(r):
        back_out[r] = through_plane(mixed[r, :half_rows]).astype(BF16)
        give_back(r).start()
        finish(r, low, through_plane(mixed[r, half_rows:]))
        give_back(r).wait_recv()
        finish(r, 1 - low, back_in[r].astype(F32))

    lax.fori_loop(0, tile_rows, prepare, 0)
    own_weights.wait()

    def await_weights(i, carry):
        take_weights(i).wait_recv()
        return carry

    def step(r, carry):
        relax(r)

        @pl.when(r == 0)
        def _():
            lax.fori_loop(1, peers, await_weights, 0)
            swap_weights(half_lanes).start()
            transport()
            swap_weights(sib_lanes).wait_recv()
            turned[...] = weights[...].T

        collide(r)
        return carry

    lax.fori_loop(0, tile_rows, step, 0)

    for r in range(tile_rows):
        for i in range(1, nh):
            for core in range(2):
                give(r, i, core).wait_send()
        give(r, 0, 1 - low).wait_send()
        give_back(r).wait_send()
    for k in range(chunks):
        store(k).wait()

    def sent(i, carry):
        send_weights(i).wait_send()
        return carry

    lax.fori_loop(1, peers, sent, 0)
    swap_weights(half_lanes).wait_send()
    for way in range(2):
        row_halo(way).wait_send()
        col_halo(way).wait_send()


def local(sizes, distribution, plane_weights, depth_weights):
    nvel, nsx, nsy = sizes
    tile_rows, tile_cols, width = distribution.shape
    depth = width // NXY
    chunks = tile_rows * tile_cols // GROUP
    packed = -(-tile_rows * depth // 16) * 16
    dma = pltpu.SemaphoreType.DMA
    cells = tile_rows * tile_cols
    return pl.pallas_call(
        functools.partial(kernel, sizes),
        out_shape=pltpu.VMEM(distribution.shape, BF16),
        in_specs=[
            pl.BlockSpec(memory_space=pl.ANY),
            pl.BlockSpec(memory_space=pl.ANY),
            pl.BlockSpec(memory_space=pltpu.VMEM),
        ],
        out_specs=pl.BlockSpec(memory_space=pl.ANY),
        scratch_shapes=[
            pltpu.VMEM((chunks, GROUP, width), BF16),
            pltpu.VMEM((nvel, tile_rows, GROUP, width), BF16),
            pltpu.VMEM((NXY, NXY), BF16),
            pltpu.VMEM((NXY, NXY), BF16),
            pltpu.VMEM((chunks, GROUP, width), F32),
            pltpu.VMEM((tile_rows, 2 * GROUP * depth, NXY), BF16),
            pltpu.VMEM((chunks, GROUP, width), BF16),
            pltpu.VMEM((2 * GROUP * depth, GROUP * NVZ), BF16),
            pltpu.VMEM((NXY, 128), BF16),
            pltpu.VMEM((tile_rows, 2 * GROUP * depth, NXY), F32),
            pltpu.VMEM((tile_rows, 3, GROUP, 128), F32),
            pltpu.VMEM((tile_rows, GROUP * depth, NXY), BF16),
            pltpu.VMEM((tile_rows, GROUP * depth, NXY), BF16),
            pltpu.VMEM((2, tile_cols, depth * HALF), BF16),
            pltpu.VMEM((2, tile_cols, depth * HALF), BF16),
            pltpu.VMEM((2, packed, NXY), BF16),
            pltpu.VMEM((2, packed, NXY), BF16),
            pltpu.VMEM((2, packed, NXY), F32),
            dma((chunks,)),
            dma((tile_rows,)),
            dma,
            dma((nvel, tile_rows)),
            dma((nvel, tile_rows)),
            dma((tile_rows,)),
            dma((tile_rows,)),
            dma((nsx * nsy,)),
            dma((nsx * nsy,)),
            dma((2,)),
            dma((4,)),
            dma((4,)),
            dma((chunks,)),
            pltpu.SemaphoreType.REGULAR,
        ],
        compiler_params=pltpu.CompilerParams(
            collective_id=0, has_side_effects=True, vmem_limit_bytes=56 * 1024 * 1024
        ),
        cost_estimate=pl.CostEstimate(
            flops=2 * cells * depth * NXY * NXY,
            bytes_accessed=4 * cells * width,
            transcendentals=cells * NXY,
        ),
    )(distribution, plane_weights, depth_weights)


def solution(mesh):
    sizes = (mesh.shape["vel"], mesh.shape["sx"], mesh.shape["sy"])
    return jax.shard_map(
        functools.partial(local, sizes),
        mesh=mesh,
        in_specs=(P("sx", "sy", "vel"), P(("sx", "sy"), None), P()),
        out_specs=P("sx", "sy", "vel"),
        check_vma=False,
    )
```
